256 devices in a mesh: site: 32 (over y, z_lo, core), ev: 8 (over x, z_hi).
Axes of the slice: x: 4, y: 4, z: 8 (z_hi: 2, z_lo: 4; z = z_hi * 4 + z_lo), core: 2. Of those that a mesh axis runs over, the one named last changes fastest.
Arguments:
- eigvecs: float32 [2, 3, 192, 32, 2304], P(None, None, 'ev', 'site'), may hold values from -0.2766705 to 0.2766705
- links: float32 [3, 2, 3, 3, 32, 2304], P(None, None, None, None, 'site'), may hold values from -3.5 to 3.5
- momenta: int32 [4, 3], replicated, may hold values from -2 to 2
- directions: int32 [3], replicated, may hold values from 0 to 2, each once
Outputs:
- elementals: float32 [4, 4, 2, 192, 192], P(None, None, None, 'site', 'ev')
The draws below stay inside these ranges and needn't reach their ends.
Inputs may be any that keep to these rules, and one draw needn't show every extreme that they name: The three directions are x, y, z in some order.
All inputs are finite; a program needn't handle non-finite values.
Results may differ from the reference program's by a relative error of at most 0.0001.
Values sent between devices are 32-bit elements; how exact they have to be, the bound alone decides.
No kernel may reach another device: no remote copies, remote signals or barrier semaphores. Data moves between devices by JAX's collectives and lax.ppermute only.
A program may use at most 128 MiB of HBM per device.

```python
import math
import jax
import jax.numpy as jnp
from jax import lax

NV = 192
LX = 48
LY = 48
MOMS = 4
NZ = 32


def place_ends(values, own_key, low, high):
    index_at = [jax.random.randint(jax.random.fold_in(own_key, axis), (), 0, length) for axis, length in enumerate(values.shape)]
    widest = values.shape.index(max(values.shape))
    neighbour = index_at[:widest] + [(index_at[widest] + 1) % values.shape[widest]] + index_at[widest + 1:]
    return values.at[tuple(index_at)].set(low).at[tuple(neighbour)].set(high)


def level_of(stream_key, extent, shards, least, high):
    def one(axis_at, shards_of):
        heights = jax.random.uniform(jax.random.fold_in(jax.random.fold_in(stream_key, 6), axis_at), (shards_of,), jnp.float32, least / len(shards), high / len(shards))
        return jnp.repeat(jnp.exp(heights), extent[axis_at] // shards_of).reshape((-1,) + (1,) * (len(extent) - axis_at - 1))

    loudness = one(*shards[0])
    for cut in shards[1:]:
        loudness = loudness * one(*cut)
    return loudness


def centred(own_key, shape, width, most, cuts=(), kind=jnp.bfloat16):
    values = jax.random.normal(own_key, shape, jnp.float32) * width
    if len(cuts) > 0:
        values = level_of(own_key, shape, cuts, -0.22, 0.18) * values
    return jnp.clip(values, min=-most, max=most).astype(kind)


def setup_inputs(seed: int = 0) -> dict:
    keys = jax.random.split(jax.random.key(seed), 5)
    return {
        "eigvecs": centred(keys[0], (2, 3, NV, NZ, LX * LY), ((3 * LX * LY * NZ) ** -0.25), 0.2766705, ((2, 8), (3, 32)), jnp.float32),
        "links": centred(keys[1], (3, 2, 3, 3, NZ, LX * LY), 0.57735, 3.5, ((4, 32),), jnp.float32),
        "momenta": place_ends(jax.random.randint(keys[2], (MOMS, 3), -2, 3), jax.random.fold_in(keys[2], 1), -2, 2).astype(jnp.int32),
        "directions": jax.random.permutation(keys[3], 3).astype(jnp.int32),
    }


def phases(momenta, zcount, xystart, xycount, ztotal):
    zpos = jnp.arange(zcount, dtype=jnp.int32)
    plane = xystart + jnp.arange(xycount, dtype=jnp.int32)
    xpos = plane // LY
    ypos = plane % LY
    px = momenta[:, 0][:, None, None]
    py = momenta[:, 1][:, None, None]
    pz = momenta[:, 2][:, None, None]
    fracx = jnp.mod(px * xpos[None, None, :], LX).astype(jnp.float32) / LX
    fracy = jnp.mod(py * ypos[None, None, :], LY).astype(jnp.float32) / LY
    fracz = jnp.mod(pz * zpos[None, :, None], ztotal).astype(jnp.float32) / ztotal
    theta = (2.0 * math.pi) * (fracx + fracy + fracz)
    return jnp.cos(theta), jnp.sin(theta)


def transport(link, far):
    real = jnp.sum(link[0][:, :, None] * far[0][None] - link[1][:, :, None] * far[1][None], axis=1)
    imag = jnp.sum(link[0][:, :, None] * far[1][None] + link[1][:, :, None] * far[0][None], axis=1)
    return jnp.stack([real, imag])


def contract(left_vector, right, cosv, sine_phase_value):
    result = []
    for momentum_index in range(cosv.shape[0]):
        cosine_value = cosv[momentum_index]
        sine_value = sine_phase_value[momentum_index]
        left_real = left_vector[0] * cosine_value - left_vector[1] * sine_value
        left_imaginary = -(left_vector[0] * sine_value + left_vector[1] * cosine_value)
        weighted = jnp.stack([left_real, left_imaginary])
        prod = jnp.einsum("acrzs,dbcjzs->abdrj", weighted, right, precision=lax.Precision.HIGHEST)
        result.append(jnp.stack([prod[0, 0] - prod[1, 1], prod[0, 1] + prod[1, 0]], axis=1))
    return jnp.stack(result)


def reference(eigvecs, links, momenta, directions):
    ztotal = eigvecs.shape[3]
    grid = eigvecs.reshape(2, 3, NV, ztotal, LX, LY)
    up_x = jnp.roll(grid, -1, axis=4).reshape(eigvecs.shape)
    up_y = jnp.roll(grid, -1, axis=5).reshape(eigvecs.shape)
    up_z = jnp.roll(eigvecs, -1, axis=3)
    moved = jnp.stack([transport(links[0], up_x), transport(links[1], up_y), transport(links[2], up_z)])
    select = (directions[:, None] == jnp.arange(3, dtype=jnp.int32)[None, :]).astype(jnp.float32)
    chosen = jnp.einsum("dk,kabjzs->dabjzs", select, moved, precision=lax.Precision.HIGHEST)
    wfield = jnp.concatenate([eigvecs[None], chosen], axis=0)
    cosv, sine_phase_value = phases(momenta, ztotal, 0, LX * LY, ztotal)
    return contract(eigvecs, wfield, cosv, sine_phase_value)
```

```python
import math

import jax
import jax.numpy as jnp
from jax import lax
from jax.experimental import pallas as pl
from jax.experimental.pallas import tpu as pltpu
from jax.sharding import Mesh
from jax.sharding import PartitionSpec as P

LY = 48
OWN = 288
WIDE = 384
KPART = 3 * WIDE
VMEM_BYTES = 56 * 1024 * 1024


def cut_kernel(vec_ref, link_ref, out_ref, link_out_ref):
    part = lax.axis_index("x") * 2 + lax.axis_index("zh")
    vec = vec_ref[...]
    link = link_ref[...]
    chosen = None
    for other in range(8):
        begin = other * OWN
        here = min(WIDE, 2304 - begin)
        piece = vec[:, begin:begin + here]
        link_piece = link[:, begin:begin + here]
        if here < WIDE:
            piece = jnp.concatenate([piece, vec[:, :WIDE - here]], axis=1)
            link_piece = jnp.concatenate([link_piece, link[:, :WIDE - here]], axis=1)
        out_ref[other] = piece
        chosen = link_piece if chosen is None else jnp.where(part == other, link_piece, chosen)
    link_out_ref[...] = chosen


def wrapped(value, period):
    rest = lax.rem(value, period)
    return jnp.where(rest < 0, rest + period, rest)


def split(value):
    high = value.astype(jnp.bfloat16)
    return high, (value - high.astype(jnp.float32)).astype(jnp.bfloat16)


def main_kernel(mom_ref, buf_ref, above_ref, link_ref, away_ref, stay_ref, whi, wlo, lhi, llo):
    core = lax.axis_index("core")
    part = lax.axis_index("x") * 2 + lax.axis_index("zh")
    zpos = lax.axis_index("y") * 8 + lax.axis_index("zl") * 2 + core
    lane = lax.broadcasted_iota(jnp.int32, (8, WIDE), 1)
    line = jnp.zeros((8, WIDE), jnp.int32)
    for step in range(1, 8):
        line = line + (lane >= step * LY).astype(jnp.int32)
    ypos = lane - line * LY
    xpos = line + part * 6
    own = lane < OWN
    last = jnp.broadcast_to((ypos == LY - 1)[:1], (48, WIDE))

    def rows(ref, xs, field):
        first = ref[2 * xs, field * 24:(field + 1) * 24, :]
        second = ref[2 * xs + 1, field * 24:(field + 1) * 24, :]
        return jnp.concatenate([first, second], axis=0)

    def put(high_ref, low_ref, row, column, value):
        high, low = split(value)
        high_ref[pl.ds(row, 48), column:column + WIDE] = high
        low_ref[pl.ds(row, 48), column:column + WIDE] = low

    def make_fields(xs, carry):
        base = pl.multiple_of(xs * 192, 16)
        plain = [rows(buf_ref, xs, field) for field in range(6)]
        for field in range(6):
            put(whi, wlo, base, field * WIDE, plain[field])
        for direction in range(3):
            if direction == 0:
                far = [pltpu.roll(value, WIDE - LY, 1) for value in plain]
            elif direction == 1:
                far = [
                    jnp.where(last, pltpu.roll(value, LY - 1, 1), pltpu.roll(value, WIDE - 1, 1))
                    for value in plain
                ]
            else:
                far = [rows(above_ref, xs, field) for field in range(6)]
            for row in range(3):
                real = None
                imag = None
                for column in range(3):
                    at = direction * 18 + row * 3 + column
                    ur = link_ref[at:at + 1, :]
                    ui = link_ref[at + 9:at + 10, :]
                    re = ur * far[column] - ui * far[3 + column]
                    im = ur * far[3 + column] + ui * far[column]
                    real = re if real is None else real + re
                    imag = im if imag is None else imag + im
                put(whi, wlo, base + 48 * (direction + 1), row * WIDE, real)
                put(whi, wlo, base + 48 * (direction + 1), KPART + row * WIDE, imag)
        return carry

    lax.fori_loop(0, 4, make_fields, 0)

    def times(left, right):
        return lax.dot_general(
            left, right, (((1,), (1,)), ((), ())), preferred_element_type=jnp.float32
        )

    for group, out_ref in ((0, away_ref), (1, stay_ref)):
        def one_momentum(index, carry, out_ref=out_ref, group=group):
            p = (2 * (1 - core) if group == 0 else 2 * core) + index
            fx = wrapped(mom_ref[p, 0] * xpos, 48).astype(jnp.float32) / 48
            fy = wrapped(mom_ref[p, 1] * ypos, 48).astype(jnp.float32) / 48
            fz = wrapped(jnp.full((8, WIDE), mom_ref[p, 2] * zpos, jnp.int32), 32).astype(jnp.float32) / 32
            theta = (2.0 * math.pi) * (fx + fy + fz)
            cosv = jnp.where(own, jnp.cos(theta), 0.0)[:1]
            sinv = jnp.where(own, jnp.sin(theta), 0.0)[:1]

            def make_left(xs, carry):
                top = pl.multiple_of(xs * 48, 16)
                low = pl.multiple_of(xs * 48 + 192, 16)
                for color in range(3):
                    a = rows(buf_ref, xs, color)
                    b = rows(buf_ref, xs, 3 + color)
                    left_real = a * cosv - b * sinv
                    left_imag = -(a * sinv + b * cosv)
                    high, rest = split(left_real)
                    lhi[pl.ds(top, 48), color * WIDE:(color + 1) * WIDE] = high
                    llo[pl.ds(top, 48), color * WIDE:(color + 1) * WIDE] = rest
                    lhi[pl.ds(low, 48), KPART + color * WIDE:KPART + (color + 1) * WIDE] = high
                    llo[pl.ds(low, 48), KPART + color * WIDE:KPART + (color + 1) * WIDE] = rest
                    high, rest = split(left_imag)
                    lhi[pl.ds(low, 48), color * WIDE:(color + 1) * WIDE] = high
                    llo[pl.ds(low, 48), color * WIDE:(color + 1) * WIDE] = rest
                    lhi[pl.ds(top, 48), KPART + color * WIDE:KPART + (color + 1) * WIDE] = -high
                    llo[pl.ds(top, 48), KPART + color * WIDE:KPART + (color + 1) * WIDE] = -rest
                return carry

            lax.fori_loop(0, 4, make_left, 0)
            left_high = lhi[...]
            left_low = llo[...]
            total = times(left_high, whi[...]) + times(left_high, wlo[...]) + times(left_low, whi[...])
            for xs in range(4):
                both = jnp.concatenate(
                    [total[:192, xs * 192:(xs + 1) * 192], total[192:, xs * 192:(xs + 1) * 192]], axis=1
                )
                for ys in range(4):
                    out_ref[xs, ys, index] = both[ys * 48:(ys + 1) * 48]
            return carry

        lax.fori_loop(0, 2, one_momentum, 0)


def gather_kernel(part_ref, out_ref):
    halves = [[], []]
    for p in range(2):
        total = part_ref[0, p]
        for source in range(1, 16):
            total = total + part_ref[source, p]
        for piece in range(8):
            for zh in range(2):
                begin = piece * 48 + zh * 24
                halves[zh].append(total[:, begin:begin + 24])
    for zh in range(2):
        packed = jnp.concatenate(halves[zh], axis=1)
        for zl in range(4):
            for core in range(2):
                begin = zl * 12 + core * 6
                out_ref[zl * 4 + zh * 2 + core, :6] = packed[begin:begin + 6]
                out_ref[zl * 4 + zh * 2 + core, 6:] = jnp.zeros((2, WIDE), jnp.float32)


def last_kernel(direction_ref, part_ref, out_ref):
    for core in range(2):
        total = part_ref[core]
        for source in range(1, 8):
            total = total + part_ref[2 * source + core]
        for p in range(2):
            for reim in range(2):
                for d in range(4):
                    begin = p * 192 + reim * 96
                    if d == 0:
                        value = total[:6, begin:begin + 24]
                    else:
                        k = direction_ref[d - 1]
                        value = total[:6, begin + 24:begin + 48]
                        for other in range(1, 3):
                            at = begin + 24 + 24 * other
                            value = jnp.where(k == other, total[:6, at:at + 24], value)
                    out_ref[2 * core + p, d, reim] = value


def vmem(count):
    return [pl.BlockSpec(memory_space=pltpu.VMEM)] * count


def local(eigvecs, links, momenta, directions):
    f32 = jnp.float32
    params = pltpu.CompilerParams(vmem_limit_bytes=VMEM_BYTES)
    smem = [pl.BlockSpec(memory_space=pltpu.SMEM)]
    cut, link = pl.pallas_call(
        cut_kernel,
        out_shape=(
            jax.ShapeDtypeStruct((8, 144, WIDE), f32),
            jax.ShapeDtypeStruct((54, WIDE), f32),
        ),
        in_specs=vmem(2),
        out_specs=tuple(vmem(2)),
        compiler_params=params,
        name="cut",
    )(eigvecs.reshape(144, 2304), links.reshape(54, 2304))
    buf = lax.all_to_all(cut, ("x", "zh"), 0, 0)
    site = ("y", "zl", "core")
    above = lax.ppermute(buf, site, [(i, (i - 1) % 32) for i in range(32)])
    away, stay = pl.pallas_call(
        main_kernel,
        out_shape=(
            jax.ShapeDtypeStruct((4, 4, 2, 48, WIDE), f32),
            jax.ShapeDtypeStruct((4, 4, 2, 48, WIDE), f32),
        ),
        in_specs=smem + vmem(3),
        out_specs=tuple(vmem(2)),
        scratch_shapes=[
            pltpu.VMEM((768, 2 * KPART), jnp.bfloat16),
            pltpu.VMEM((768, 2 * KPART), jnp.bfloat16),
            pltpu.VMEM((384, 2 * KPART), jnp.bfloat16),
            pltpu.VMEM((384, 2 * KPART), jnp.bfloat16),
        ],
        compiler_params=params,
        name="contract",
    )(momenta, buf, above, link)
    stay = stay + lax.ppermute(away, "core", [(0, 1), (1, 0)])
    parts = lax.all_to_all(stay.reshape(16, 2, 48, WIDE), ("x", "y"), 0, 0)
    packed = pl.pallas_call(
        gather_kernel,
        out_shape=jax.ShapeDtypeStruct((16, 8, WIDE), f32),
        in_specs=vmem(1),
        out_specs=vmem(1)[0],
        compiler_params=params,
        name="gather",
    )(parts)
    parts = lax.all_to_all(packed, ("zl", "zh", "core"), 0, 0)
    return pl.pallas_call(
        last_kernel,
        out_shape=jax.ShapeDtypeStruct((4, 4, 2, 6, 24), f32),
        in_specs=smem + vmem(1),
        out_specs=vmem(1)[0],
        compiler_params=params,
        name="last",
    )(directions, parts)


def solution(mesh):
    fine = Mesh(mesh.devices.reshape(4, 4, 2, 4, 2), ("y", "zl", "core", "x", "zh"))
    site = ("y", "zl", "core")
    ev = ("x", "zh")
    in_specs = (P(None, None, ev, site, None), P(None, None, None, None, site, None), P(), P())
    out_specs = P(None, None, None, site, ev)
    return jax.shard_map(local, mesh=fine, in_specs=in_specs, out_specs=out_specs, check_vma=False)
```

```python
import math

import jax
import jax.numpy as jnp
from jax import lax
from jax.experimental import pallas as pl
from jax.experimental.pallas import tpu as pltpu
from jax.sharding import Mesh
from jax.sharding import PartitionSpec as P

LY = 48
OWN = 288
TAIL = 32
ROWS = 384
DEPTH = 896
TAIL_ROW = 288
FAR_ROW = 336
VMEM_BYTES = 40 * 1024 * 1024


def cut_kernel(vec_ref, link_ref, out_ref, link_out_ref):
    part = lax.axis_index("x") * 2 + lax.axis_index("zh")
    for other in range(8):
        begin = other * OWN
        halo = (begin + OWN) % 2304
        out_ref[other, 0:144] = vec_ref[:, begin:begin + 128]
        out_ref[other, 144:288] = vec_ref[:, begin + 128:begin + 256]
        for reim in range(2):
            tails = []
            firsts = []
            lasts = []
            for color in range(3):
                row = (reim * 3 + color) * 24
                tails.append(vec_ref[row:row + 24, begin + 256:begin + 288])
                firsts.append(vec_ref[row:row + 24, halo:halo + 16])
                lasts.append(vec_ref[row:row + 24, halo + 16:halo + 48])
            row = TAIL_ROW + reim * 24
            out_ref[other, row:row + 24] = jnp.concatenate(tails + firsts[:2], axis=1)
            row = FAR_ROW + reim * 24
            out_ref[other, row:row + 24] = jnp.concatenate(
                lasts + [firsts[2], firsts[2]], axis=1
            )
    link = link_ref[...]
    chosen = None
    for other in range(8):
        begin = other * OWN
        piece = link[:, begin:begin + OWN]
        chosen = piece if chosen is None else jnp.where(part == other, piece, chosen)
    link_out_ref[0, :54] = chosen[:, :128]
    link_out_ref[1, :54] = chosen[:, 128:256]
    tail = chosen[:, 256:288]
    for first in range(6):
        for turn in range(3):
            pieces = []
            for row in range(3):
                at = first * 9 + row * 3 + (row + turn) % 3
                pieces.append(tail[at:at + 1])
            pieces.append(jnp.zeros((1, 32), jnp.float32))
            at = first * 3 + turn
            link_out_ref[2, at:at + 1] = jnp.concatenate(pieces, axis=1)


def wrapped(value, period):
    rest = lax.rem(value, period)
    return jnp.where(rest < 0, rest + period, rest)


def split(value):
    high = value.astype(jnp.bfloat16)
    return high, (value - high.astype(jnp.float32)).astype(jnp.bfloat16)


def lanes(rows=48):
    return lax.broadcasted_iota(jnp.int32, (rows, 128), 1)


def tiles_of(ref, xs):
    def rows(row):
        return jnp.concatenate([ref[2 * xs, row:row + 24], ref[2 * xs + 1, row:row + 24]], axis=0)

    return [
        [
            [rows((reim * 3 + color) * 24) for color in range(3)]
            + [rows(144 + (reim * 3 + color) * 24) for color in range(3)]
            + [rows(TAIL_ROW + reim * 24)]
        ][0]
        for reim in range(2)
    ]


def put_tiles(high_ref, low_ref, row, tiles):
    for index, value in enumerate(tiles):
        high, low = split(value)
        column = (2 * index if index < 3 else 2 * (index - 3) + 1) * 128 if index < 6 else 768
        high_ref[pl.ds(row, 48), column:column + 128] = high
        low_ref[pl.ds(row, 48), column:column + 128] = low


def beyond_x(tiles, far):
    lane = lanes()
    low, high, tail = tiles[:3], tiles[3:6], tiles[6]
    result = []
    for color in range(3):
        result.append(jnp.where(lane < 80, pltpu.roll(low[color], 80, 1), pltpu.roll(high[color], 80, 1)))
    for color in range(3):
        own = pltpu.roll(tail, (80 - 32 * color) % 128, 1)
        if color == 0:
            first = pltpu.roll(tail, 16, 1)
        elif color == 1:
            first = tail
        else:
            first = pltpu.roll(far, 16, 1)
        value = jnp.where(lane < 80, pltpu.roll(high[color], 80, 1), own)
        result.append(jnp.where(lane < 112, value, first))
    result.append(far)
    return result


def beyond_y(tiles):
    lane = lanes()
    low, high, tail = tiles[:3], tiles[3:6], tiles[6]
    result = []
    for color in range(3):
        value = pltpu.roll(low[color], 127, 1)
        value = jnp.where((lane == 47) | (lane == 95), pltpu.roll(low[color], 47, 1), value)
        result.append(jnp.where(lane == 127, pltpu.roll(high[color], 127, 1), value))
    for color in range(3):
        value = pltpu.roll(high[color], 127, 1)
        value = jnp.where((lane == 63) | (lane == 111), pltpu.roll(high[color], 47, 1), value)
        value = jnp.where(lane == 15, pltpu.roll(low[color], 47, 1), value)
        result.append(jnp.where(lane == 127, pltpu.roll(tail, (127 - 32 * color) % 128, 1), value))
    value = pltpu.roll(tail, 127, 1)
    for color in range(3):
        at = 32 * color + 31
        value = jnp.where(lane == at, pltpu.roll(high[color], (at - 112) % 128, 1), value)
    result.append(value)
    return result


def turned(tail, turn):
    lane = lanes()
    if turn == 0:
        return tail
    if turn == 1:
        return jnp.where(lane < 64, pltpu.roll(tail, 96, 1), pltpu.roll(tail, 64, 1))
    return jnp.where(lane < 32, pltpu.roll(tail, 64, 1), pltpu.roll(tail, 32, 1))


def moved(real, imag, link_ref, direction):
    out_real = []
    out_imag = []
    for half in range(2):
        for row in range(3):
            re = None
            im = None
            for column in range(3):
                at = direction * 18 + row * 3 + column
                ur = link_ref[half, at:at + 1, :]
                ui = link_ref[half, at + 9:at + 10, :]
                fr = real[3 * half + column]
                fi = imag[3 * half + column]
                more_re = ur * fr - ui * fi
                more_im = ur * fi + ui * fr
                re = more_re if re is None else re + more_re
                im = more_im if im is None else im + more_im
            out_real.append(re)
            out_imag.append(im)
    re = None
    im = None
    for turn in range(3):
        at = direction * 6 + turn
        ur = link_ref[2, at:at + 1, :]
        ui = link_ref[2, at + 3:at + 4, :]
        fr = turned(real[6], turn)
        fi = turned(imag[6], turn)
        more_re = ur * fr - ui * fi
        more_im = ur * fi + ui * fr
        re = more_re if re is None else re + more_re
        im = more_im if im is None else im + more_im
    out_real.append(re)
    out_imag.append(im)
    return out_real, out_imag


def contract(chunk, mom_ref, buf_ref, above_ref, link_ref, away_ref, stay_ref, whi, wlo, lhi, llo):
    core = lax.axis_index("core")
    part = lax.axis_index("x") * 2 + lax.axis_index("zh")
    zpos = lax.axis_index("y") * 8 + lax.axis_index("zl") * 2 + core

    def make_fields(xs, carry):
        base = pl.multiple_of(xs * 96, 16)
        real, imag = tiles_of(buf_ref, xs)
        if chunk == 0:
            far = [
                jnp.concatenate([buf_ref[2 * xs, row:row + 24], buf_ref[2 * xs + 1, row:row + 24]], axis=0)
                for row in (FAR_ROW, FAR_ROW + 24)
            ]
            first = (real, imag)
            second = moved(beyond_x(real, far[0]), beyond_x(imag, far[1]), link_ref, 0)
        else:
            first = moved(beyond_y(real), beyond_y(imag), link_ref, 1)
            second = moved(*tiles_of(above_ref, xs), link_ref, 2)
        for k, field in enumerate((first, second)):
            for reim in range(2):
                put_tiles(whi, wlo, base + reim * 384 + k * 48, field[reim])
        return carry

    lax.fori_loop(0, 4, make_fields, 0)

    lane = lanes(8)
    sites = [lane, lane + 128, 256 + lax.rem(lane, 32)]
    lines = []
    for site in sites:
        line = jnp.zeros((8, 128), jnp.int32)
        for step in range(1, 6):
            line = line + (site >= step * LY).astype(jnp.int32)
        lines.append(line)

    def times(left, right):
        return lax.dot_general(
            left, right, (((1,), (1,)), ((), ())), preferred_element_type=jnp.float32
        )

    for group, out_ref in ((0, away_ref), (1, stay_ref)):
        for index in range(2):
            p = (2 * (1 - core) if group == 0 else 2 * core) + index
            phase = []
            for at in range(3):
                xpos = lines[at] + part * 6
                ypos = sites[at] - lines[at] * LY
                fx = wrapped(mom_ref[p, 0] * xpos, 48).astype(jnp.float32) / 48
                fy = wrapped(mom_ref[p, 1] * ypos, 48).astype(jnp.float32) / 48
                fz = wrapped(jnp.full((8, 128), mom_ref[p, 2] * zpos, jnp.int32), 32)
                theta = (2.0 * math.pi) * (fx + fy + fz.astype(jnp.float32) / 32)
                cosv = jnp.cos(theta)
                sinv = jnp.sin(theta)
                if at == 2:
                    cosv = jnp.where(lane < 96, cosv, 0.0)
                    sinv = jnp.where(lane < 96, sinv, 0.0)
                phase.append((cosv[:1], sinv[:1]))

            def make_left(xs, carry, phase=phase):
                top = pl.multiple_of(xs * 48, 16)
                real, imag = tiles_of(buf_ref, xs)
                left_real = []
                left_imag = []
                for at in range(7):
                    cosv, sinv = phase[at // 3]
                    left_real.append(real[at] * cosv - imag[at] * sinv)
                    left_imag.append(-(real[at] * sinv + imag[at] * cosv))
                put_tiles(lhi, llo, top, left_real)
                put_tiles(lhi, llo, top + 192, left_imag)
                return carry

            lax.fori_loop(0, 4, make_left, 0)
            left_high = lhi[...]
            left_low = llo[...]
            total = times(left_high, whi[...]) + times(left_high, wlo[...]) + times(left_low, whi[...])
            product = (
                total[:192, :384] - total[192:, 384:],
                total[192:, :384] + total[:192, 384:],
            )
            for reim in range(2):
                column = (2 * index + reim) * 96
                for xs in range(4):
                    value = product[reim][:, xs * 96:(xs + 1) * 96]
                    for ys in range(4):
                        out_ref[xs, ys, :, column:column + 96] = value[ys * 48:(ys + 1) * 48]


def first_kernel(mom_ref, buf_ref, link_ref, away_ref, stay_ref, *scratch):
    contract(0, mom_ref, buf_ref, None, link_ref, away_ref, stay_ref, *scratch)


def second_kernel(mom_ref, buf_ref, above_ref, link_ref, away_ref, stay_ref, *scratch):
    contract(1, mom_ref, buf_ref, above_ref, link_ref, away_ref, stay_ref, *scratch)


def add_kernel(stay_ref, came_ref, *out_refs):
    mine = {"y": lax.axis_index("y"), "x": lax.axis_index("x")}
    for step in range(4):
        to_y = lax.rem(mine["y"] + step, 4)
        to_x = lax.rem(mine["x"] + step, 4)
        for other in range(4):
            out_refs[step][other] = stay_ref[other, to_y, :24] + came_ref[other, to_y, :24]
            out_refs[4 + step][other] = stay_ref[to_x, other, 24:] + came_ref[to_x, other, 24:]


def sum_kernel(*refs):
    ins, outs = refs[:16], refs[16:]
    mine = (lax.axis_index("x"), lax.axis_index("y"))
    for chunk in range(2):
        for half in range(2):
            group = ins[chunk * 8 + half * 4:chunk * 8 + half * 4 + 4]
            for step in range(4):
                to = lax.rem(mine[half] + step, 4)
                total = group[0][to]
                for source in range(1, 4):
                    total = total + group[source][to]
                outs[half * 4 + step][chunk] = total


def gather_kernel(*refs):
    ins, out_ref = refs[:8], refs[8]
    for half in range(2):
        pieces = [[], []]
        for chunk in range(2):
            total = ins[4 * half][chunk]
            for source in range(1, 4):
                total = total + ins[4 * half + source][chunk]
            for piece in range(8):
                for zh in range(2):
                    begin = piece * 48 + zh * 24
                    pieces[zh].append(total[:, begin:begin + 24])
        for zh in range(2):
            packed = jnp.concatenate(pieces[zh], axis=1)
            for zl in range(2):
                for core in range(2):
                    begin = zl * 12 + core * 6
                    to = (2 * half + zl) * 4 + zh * 2 + core
                    out_ref[to, :6] = packed[begin:begin + 6]
                    out_ref[to, 6:] = jnp.zeros((2, 384), jnp.float32)


def last_kernel(direction_ref, part_ref, out_ref):
    for core in range(2):
        total = part_ref[core]
        for source in range(1, 8):
            total = total + part_ref[2 * source + core]
        total = total[:6]
        for p in range(2):
            for reim in range(2):
                begin = p * 96 + reim * 48
                fields = []
                for field in range(4):
                    at = begin + (field // 2) * 192 + (field % 2) * 24
                    fields.append(total[:, at:at + 24])
                out_ref[2 * core + p, 0, reim] = fields[0]
                for d in range(1, 4):
                    k = direction_ref[d - 1]
                    value = jnp.where(k == 1, fields[2], fields[1])
                    out_ref[2 * core + p, d, reim] = jnp.where(k == 2, fields[3], value)


def vmem(count):
    return [pl.BlockSpec(memory_space=pltpu.VMEM)] * count


def call(kernel, name, out_shapes, operands, scratch=(), scalars=0):
    out_shape = tuple(jax.ShapeDtypeStruct(shape, jnp.float32) for shape in out_shapes)
    return pl.pallas_call(
        kernel,
        out_shape=out_shape,
        in_specs=[pl.BlockSpec(memory_space=pltpu.SMEM)] * scalars + vmem(len(operands) - scalars),
        out_specs=tuple(vmem(len(out_shapes))),
        scratch_shapes=list(scratch),
        compiler_params=pltpu.CompilerParams(vmem_limit_bytes=VMEM_BYTES),
        name=name,
    )(*operands)


def around(value, axis, step):
    return lax.ppermute(value, axis, [(i, (i + step) % 4) for i in range(4)])


def local(eigvecs, links, momenta, directions):
    cut, link = call(
        cut_kernel, "cut", [(8, ROWS, 128), (3, 56, 128)],
        (eigvecs.reshape(144, 2304), links.reshape(54, 2304)),
    )
    buf = lax.all_to_all(cut, ("x", "zh"), 0, 0)
    above = lax.ppermute(buf, ("y", "zl", "core"), [(i, (i - 1) % 32) for i in range(32)])
    scratch = [pltpu.VMEM((768, DEPTH), jnp.bfloat16)] * 2 + [pltpu.VMEM((384, DEPTH), jnp.bfloat16)] * 2
    sums = []
    for chunk in range(2):
        away, stay = call(
            (first_kernel, second_kernel)[chunk], ("contract_vx", "contract_yz")[chunk],
            [(4, 4, 48, 384)] * 2,
            (momenta, buf, link) if chunk == 0 else (momenta, buf, above, link),
            scratch, 1,
        )
        came = lax.ppermute(away, "core", [(0, 1), (1, 0)])
        ready = call(add_kernel, "add", [(4, 24, 384)] * 8, (stay, came))
        sums += [ready[0]] + [around(ready[step], "y", step) for step in range(1, 4)]
        sums += [ready[4]] + [around(ready[4 + step], "x", step) for step in range(1, 4)]
    ready = call(sum_kernel, "sum", [(2, 24, 384)] * 8, sums)
    sums = [ready[0]] + [around(ready[step], "x", step) for step in range(1, 4)]
    sums += [ready[4]] + [around(ready[4 + step], "y", step) for step in range(1, 4)]
    packed, = call(gather_kernel, "gather", [(16, 8, 384)], sums)
    parts = lax.all_to_all(packed, ("zl", "zh", "core"), 0, 0)
    return call(last_kernel, "last", [(4, 4, 2, 6, 24)], (directions, parts), (), 1)[0]


def solution(mesh):
    fine = Mesh(mesh.devices.reshape(4, 4, 2, 4, 2), ("y", "zl", "core", "x", "zh"))
    site = ("y", "zl", "core")
    ev = ("x", "zh")
    in_specs = (P(None, None, ev, site, None), P(None, None, None, None, site, None), P(), P())
    out_specs = P(None, None, None, site, ev)
    return jax.shard_map(local, mesh=fine, in_specs=in_specs, out_specs=out_specs, check_vma=False)
```

```python
import math

import jax
import jax.numpy as jnp
from jax import lax
from jax.experimental import pallas as pl
from jax.experimental.pallas import tpu as pltpu
from jax.sharding import Mesh
from jax.sharding import PartitionSpec as P

LY = 48
OWN = 288
TAIL = 32
ROWS = 384
DEPTH = 896
TAIL_ROW = 288
FAR_ROW = 336
VMEM_BYTES = 40 * 1024 * 1024


def cut_kernel(vec_ref, link_ref, out_ref, link_out_ref):
    part = lax.axis_index("x") * 2 + lax.axis_index("zh")
    for other in range(8):
        begin = other * OWN
        halo = (begin + OWN) % 2304
        out_ref[other, 0:144] = vec_ref[:, begin:begin + 128]
        out_ref[other, 144:288] = vec_ref[:, begin + 128:begin + 256]
        for reim in range(2):
            tails = []
            firsts = []
            lasts = []
            for color in range(3):
                row = (reim * 3 + color) * 24
                tails.append(vec_ref[row:row + 24, begin + 256:begin + 288])
                firsts.append(vec_ref[row:row + 24, halo:halo + 16])
                lasts.append(vec_ref[row:row + 24, halo + 16:halo + 48])
            row = TAIL_ROW + reim * 24
            out_ref[other, row:row + 24] = jnp.concatenate(tails + firsts[:2], axis=1)
            row = FAR_ROW + reim * 24
            out_ref[other, row:row + 24] = jnp.concatenate(
                lasts + [firsts[2], firsts[2]], axis=1
            )
    link = link_ref[...]
    chosen = None
    for other in range(8):
        begin = other * OWN
        piece = link[:, begin:begin + OWN]
        chosen = piece if chosen is None else jnp.where(part == other, piece, chosen)
    link_out_ref[0, :54] = chosen[:, :128]
    link_out_ref[1, :54] = chosen[:, 128:256]
    tail = chosen[:, 256:288]
    for first in range(6):
        for turn in range(3):
            pieces = []
            for row in range(3):
                at = first * 9 + row * 3 + (row + turn) % 3
                pieces.append(tail[at:at + 1])
            pieces.append(jnp.zeros((1, 32), jnp.float32))
            at = first * 3 + turn
            link_out_ref[2, at:at + 1] = jnp.concatenate(pieces, axis=1)


def wrapped(value, period):
    rest = lax.rem(value, period)
    return jnp.where(rest < 0, rest + period, rest)


def split(value):
    high = value.astype(jnp.bfloat16)
    return high, (value - high.astype(jnp.float32)).astype(jnp.bfloat16)


def lanes(rows=48):
    return lax.broadcasted_iota(jnp.int32, (rows, 128), 1)


def tiles_of(ref, xs):
    def rows(row):
        return jnp.concatenate([ref[2 * xs, row:row + 24], ref[2 * xs + 1, row:row + 24]], axis=0)

    return [
        [
            [rows((reim * 3 + color) * 24) for color in range(3)]
            + [rows(144 + (reim * 3 + color) * 24) for color in range(3)]
            + [rows(TAIL_ROW + reim * 24)]
        ][0]
        for reim in range(2)
    ]


def put_tiles(high_ref, low_ref, row, tiles):
    for index, value in enumerate(tiles):
        high, low = split(value)
        column = (2 * index if index < 3 else 2 * (index - 3) + 1) * 128 if index < 6 else 768
        high_ref[pl.ds(row, 48), column:column + 128] = high
        low_ref[pl.ds(row, 48), column:column + 128] = low


def beyond_x(tiles, far):
    lane = lanes()
    low, high, tail = tiles[:3], tiles[3:6], tiles[6]
    result = []
    for color in range(3):
        result.append(jnp.where(lane < 80, pltpu.roll(low[color], 80, 1), pltpu.roll(high[color], 80, 1)))
    for color in range(3):
        own = pltpu.roll(tail, (80 - 32 * color) % 128, 1)
        if color == 0:
            first = pltpu.roll(tail, 16, 1)
        elif color == 1:
            first = tail
        else:
            first = pltpu.roll(far, 16, 1)
        value = jnp.where(lane < 80, pltpu.roll(high[color], 80, 1), own)
        result.append(jnp.where(lane < 112, value, first))
    result.append(far)
    return result


def beyond_y(tiles):
    lane = lanes()
    low, high, tail = tiles[:3], tiles[3:6], tiles[6]
    result = []
    for color in range(3):
        value = pltpu.roll(low[color], 127, 1)
        value = jnp.where((lane == 47) | (lane == 95), pltpu.roll(low[color], 47, 1), value)
        result.append(jnp.where(lane == 127, pltpu.roll(high[color], 127, 1), value))
    for color in range(3):
        value = pltpu.roll(high[color], 127, 1)
        value = jnp.where((lane == 63) | (lane == 111), pltpu.roll(high[color], 47, 1), value)
        value = jnp.where(lane == 15, pltpu.roll(low[color], 47, 1), value)
        result.append(jnp.where(lane == 127, pltpu.roll(tail, (127 - 32 * color) % 128, 1), value))
    value = pltpu.roll(tail, 127, 1)
    for color in range(3):
        at = 32 * color + 31
        value = jnp.where(lane == at, pltpu.roll(high[color], (at - 112) % 128, 1), value)
    result.append(value)
    return result


def turned(tail, turn):
    lane = lanes()
    if turn == 0:
        return tail
    if turn == 1:
        return jnp.where(lane < 64, pltpu.roll(tail, 96, 1), pltpu.roll(tail, 64, 1))
    return jnp.where(lane < 32, pltpu.roll(tail, 64, 1), pltpu.roll(tail, 32, 1))


def moved(real, imag, link_ref, direction):
    out_real = []
    out_imag = []
    for half in range(2):
        for row in range(3):
            re = None
            im = None
            for column in range(3):
                at = direction * 18 + row * 3 + column
                ur = link_ref[half, at:at + 1, :]
                ui = link_ref[half, at + 9:at + 10, :]
                fr = real[3 * half + column]
                fi = imag[3 * half + column]
                more_re = ur * fr - ui * fi
                more_im = ur * fi + ui * fr
                re = more_re if re is None else re + more_re
                im = more_im if im is None else im + more_im
            out_real.append(re)
            out_imag.append(im)
    re = None
    im = None
    for turn in range(3):
        at = direction * 6 + turn
        ur = link_ref[2, at:at + 1, :]
        ui = link_ref[2, at + 3:at + 4, :]
        fr = turned(real[6], turn)
        fi = turned(imag[6], turn)
        more_re = ur * fr - ui * fi
        more_im = ur * fi + ui * fr
        re = more_re if re is None else re + more_re
        im = more_im if im is None else im + more_im
    out_real.append(re)
    out_imag.append(im)
    return out_real, out_imag


def contract(chunk, mom_ref, buf_ref, above_ref, link_ref, away_ref, stay_ref, whi, wlo, lhi, llo):
    core = lax.axis_index("core")
    part = lax.axis_index("x") * 2 + lax.axis_index("zh")
    zpos = lax.axis_index("y") * 8 + lax.axis_index("zl") * 2 + core

    def make_fields(xs, carry):
        base = pl.multiple_of(xs * 96, 16)
        real, imag = tiles_of(buf_ref, xs)
        if chunk == 0:
            far = [
                jnp.concatenate([buf_ref[2 * xs, row:row + 24], buf_ref[2 * xs + 1, row:row + 24]], axis=0)
                for row in (FAR_ROW, FAR_ROW + 24)
            ]
            first = (real, imag)
            second = moved(beyond_x(real, far[0]), beyond_x(imag, far[1]), link_ref, 0)
        else:
            first = moved(beyond_y(real), beyond_y(imag), link_ref, 1)
            second = moved(*tiles_of(above_ref, xs), link_ref, 2)
        for k, field in enumerate((first, second)):
            for reim in range(2):
                put_tiles(whi, wlo, base + reim * 384 + k * 48, field[reim])
        return carry

    lax.fori_loop(0, 4, make_fields, 0)

    row = lax.broadcasted_iota(jnp.int32, (16, 128), 0)
    lane = lanes(16)
    site = jnp.where(row < 4, lane, jnp.where(row < 8, lane + 128, 256 + (lane & 31)))
    line = jnp.zeros((16, 128), jnp.int32)
    for step in range(1, 6):
        line = line + (site >= step * LY).astype(jnp.int32)
    momentum = []
    for axis in range(3):
        value = jnp.zeros((16, 128), jnp.int32)
        for at in range(12):
            p = (2 * (1 - core) if at % 4 < 2 else 2 * core) + at % 2
            value = jnp.where(row == at, mom_ref[p, axis], value)
        momentum.append(value)
    fx = wrapped(momentum[0] * (line + part * 6), 48).astype(jnp.float32) / 48
    fy = wrapped(momentum[1] * (site - line * LY), 48).astype(jnp.float32) / 48
    fz = wrapped(momentum[2] * zpos, 32).astype(jnp.float32) / 32
    theta = (2.0 * math.pi) * (fx + fy + fz)
    used = (row < 8) | (lane < 96)
    cosines = jnp.where(used, jnp.cos(theta), 0.0)
    sines = jnp.where(used, jnp.sin(theta), 0.0)

    def make_left(xs, carry):
        top = pl.multiple_of(xs * 48, 16)
        real, imag = tiles_of(buf_ref, xs)
        for index in range(4):
            left_real = []
            left_imag = []
            for at in range(7):
                row = 4 * (at // 3) + index
                cosv = cosines[row:row + 1]
                sinv = sines[row:row + 1]
                left_real.append(real[at] * cosv - imag[at] * sinv)
                left_imag.append(-(real[at] * sinv + imag[at] * cosv))
            put_tiles(lhi.at[index], llo.at[index], top, left_real)
            put_tiles(lhi.at[index], llo.at[index], top + 192, left_imag)
        return carry

    lax.fori_loop(0, 4, make_left, 0)

    def times(left, right):
        return lax.dot_general(
            left, right, (((1,), (1,)), ((), ())), preferred_element_type=jnp.float32
        )

    for index in range(4):
        out_ref = (away_ref, stay_ref)[index // 2]
        total = (
            times(lhi[index], whi[...]) + times(lhi[index], wlo[...]) + times(llo[index], whi[...])
        )
        product = (
            total[:192, :384] - total[192:, 384:],
            total[192:, :384] + total[:192, 384:],
        )
        for reim in range(2):
            column = (2 * (index % 2) + reim) * 96
            for xs in range(4):
                value = product[reim][:, xs * 96:(xs + 1) * 96]
                for ys in range(4):
                    out_ref[xs, ys, :, column:column + 96] = value[ys * 48:(ys + 1) * 48]


def first_kernel(mom_ref, buf_ref, link_ref, away_ref, stay_ref, *scratch):
    contract(0, mom_ref, buf_ref, None, link_ref, away_ref, stay_ref, *scratch)


def second_kernel(mom_ref, buf_ref, above_ref, link_ref, away_ref, stay_ref, *scratch):
    contract(1, mom_ref, buf_ref, above_ref, link_ref, away_ref, stay_ref, *scratch)


def add_kernel(stay_ref, came_ref, *out_refs):
    mine = {"y": lax.axis_index("y"), "x": lax.axis_index("x")}
    for step in range(4):
        to_y = lax.rem(mine["y"] + step, 4)
        to_x = lax.rem(mine["x"] + step, 4)
        for other in range(4):
            out_refs[step][other] = stay_ref[other, to_y, :24] + came_ref[other, to_y, :24]
            out_refs[4 + step][other] = stay_ref[to_x, other, 24:] + came_ref[to_x, other, 24:]


def sum_kernel(*refs):
    ins, outs = refs[:16], refs[16:]
    mine = (lax.axis_index("x"), lax.axis_index("y"))
    for chunk in range(2):
        for half in range(2):
            group = ins[chunk * 8 + half * 4:chunk * 8 + half * 4 + 4]
            for step in range(4):
                to = lax.rem(mine[half] + step, 4)
                total = group[0][to]
                for source in range(1, 4):
                    total = total + group[source][to]
                outs[half * 4 + step][chunk] = total


def gather_kernel(*refs):
    ins, out_ref = refs[:8], refs[8]
    for half in range(2):
        pieces = [[], []]
        for chunk in range(2):
            total = ins[4 * half][chunk]
            for source in range(1, 4):
                total = total + ins[4 * half + source][chunk]
            for piece in range(8):
                for zh in range(2):
                    begin = piece * 48 + zh * 24
                    pieces[zh].append(total[:, begin:begin + 24])
        for zh in range(2):
            packed = jnp.concatenate(pieces[zh], axis=1)
            for zl in range(2):
                for core in range(2):
                    begin = zl * 12 + core * 6
                    to = (2 * half + zl) * 4 + zh * 2 + core
                    out_ref[to, :6] = packed[begin:begin + 6]
                    out_ref[to, 6:] = jnp.zeros((2, 384), jnp.float32)


def last_kernel(direction_ref, part_ref, out_ref):
    for core in range(2):
        total = part_ref[core]
        for source in range(1, 8):
            total = total + part_ref[2 * source + core]
        total = total[:6]
        for p in range(2):
            for reim in range(2):
                begin = p * 96 + reim * 48
                fields = []
                for field in range(4):
                    at = begin + (field // 2) * 192 + (field % 2) * 24
                    fields.append(total[:, at:at + 24])
                out_ref[2 * core + p, 0, reim] = fields[0]
                for d in range(1, 4):
                    k = direction_ref[d - 1]
                    value = jnp.where(k == 1, fields[2], fields[1])
                    out_ref[2 * core + p, d, reim] = jnp.where(k == 2, fields[3], value)


def vmem(count):
    return [pl.BlockSpec(memory_space=pltpu.VMEM)] * count


def call(kernel, name, out_shapes, operands, scratch=(), scalars=0):
    out_shape = tuple(jax.ShapeDtypeStruct(shape, jnp.float32) for shape in out_shapes)
    return pl.pallas_call(
        kernel,
        out_shape=out_shape,
        in_specs=[pl.BlockSpec(memory_space=pltpu.SMEM)] * scalars + vmem(len(operands) - scalars),
        out_specs=tuple(vmem(len(out_shapes))),
        scratch_shapes=list(scratch),
        compiler_params=pltpu.CompilerParams(vmem_limit_bytes=VMEM_BYTES),
        name=name,
    )(*operands)


def around(value, axis, step):
    return lax.ppermute(value, axis, [(i, (i + step) % 4) for i in range(4)])


def local(eigvecs, links, momenta, directions):
    cut, link = call(
        cut_kernel, "cut", [(8, ROWS, 128), (3, 56, 128)],
        (eigvecs.reshape(144, 2304), links.reshape(54, 2304)),
    )
    buf = lax.all_to_all(cut, ("x", "zh"), 0, 0)
    above = lax.ppermute(buf, ("y", "zl", "core"), [(i, (i - 1) % 32) for i in range(32)])
    scratch = [pltpu.VMEM((768, DEPTH), jnp.bfloat16)] * 2 + [pltpu.VMEM((4, 384, DEPTH), jnp.bfloat16)] * 2
    sums = []
    for chunk in range(2):
        away, stay = call(
            (first_kernel, second_kernel)[chunk], ("contract_vx", "contract_yz")[chunk],
            [(4, 4, 48, 384)] * 2,
            (momenta, buf, link) if chunk == 0 else (momenta, buf, above, link),
            scratch, 1,
        )
        came = lax.ppermute(away, "core", [(0, 1), (1, 0)])
        ready = call(add_kernel, "add", [(4, 24, 384)] * 8, (stay, came))
        sums += [ready[0]] + [around(ready[step], "y", step) for step in range(1, 4)]
        sums += [ready[4]] + [around(ready[4 + step], "x", step) for step in range(1, 4)]
    ready = call(sum_kernel, "sum", [(2, 24, 384)] * 8, sums)
    sums = [ready[0]] + [around(ready[step], "x", step) for step in range(1, 4)]
    sums += [ready[4]] + [around(ready[4 + step], "y", step) for step in range(1, 4)]
    packed, = call(gather_kernel, "gather", [(16, 8, 384)], sums)
    parts = lax.all_to_all(packed, ("zl", "zh", "core"), 0, 0)
    return call(last_kernel, "last", [(4, 4, 2, 6, 24)], (directions, parts), (), 1)[0]


def solution(mesh):
    fine = Mesh(mesh.devices.reshape(4, 4, 2, 4, 2), ("y", "zl", "core", "x", "zh"))
    site = ("y", "zl", "core")
    ev = ("x", "zh")
    in_specs = (P(None, None, ev, site, None), P(None, None, None, None, site, None), P(), P())
    out_specs = P(None, None, None, site, ev)
    return jax.shard_map(local, mesh=fine, in_specs=in_specs, out_specs=out_specs, check_vma=False)
```

```python
import math

import jax
import jax.numpy as jnp
from jax import lax
from jax.experimental import pallas as pl
from jax.experimental.pallas import tpu as pltpu
from jax.sharding import Mesh
from jax.sharding import PartitionSpec as P

LY = 48
HALF = 1152
TILES = 9
ROWS = 1296
DEPTH = 3456
SITE = ("y", "zl", "core")
VMEM_BYTES = 44 * 1024 * 1024


def cut_kernel(vec_ref, link_ref, keep_ref, send_ref, halo_ref, halo_send_ref, link_out_ref):
    zh = lax.axis_index("zh")
    for out_ref, other_ref, begin in ((keep_ref, halo_send_ref, zh), (send_ref, halo_ref, 1 - zh)):
        for tile in range(TILES):
            at = pl.ds(pl.multiple_of(begin * HALF + tile * 128, 128), 128)
            for reim in range(2):
                row = reim * 648 + tile * 72
                out_ref[row:row + 72] = vec_ref[reim * 72:reim * 72 + 72, at]
        lane = lax.broadcasted_iota(jnp.int32, (24, 128), 1)
        at = pl.ds(pl.multiple_of(begin * HALF, 128), 128)
        for pair in range(3):
            even = vec_ref[pair * 48:pair * 48 + 24, at]
            odd = vec_ref[pair * 48 + 24:pair * 48 + 48, at]
            other_ref[pair * 24:pair * 24 + 24] = jnp.where(lane < LY, even, pltpu.roll(odd, LY, 1))
    for tile in range(TILES):
        at = pl.ds(pl.multiple_of(zh * HALF + tile * 128, 128), 128)
        link_out_ref[tile, :54] = link_ref[:, at]


def wrapped(value, period):
    rest = lax.rem(value, period)
    return jnp.where(rest < 0, rest + period, rest)


def phase_kernel(mom_ref, out_ref):
    core = lax.axis_index("core")
    zpos = lax.axis_index("y") * 8 + lax.axis_index("zl") * 2 + core
    row = lax.broadcasted_iota(jnp.int32, (40, 128), 0)
    site = lax.broadcasted_iota(jnp.int32, (40, 128), 1) + 128 * (row >> 2)
    line = jnp.floor((site.astype(jnp.float32) + 0.5) * (1.0 / LY)).astype(jnp.int32)
    momentum = []
    for axis in range(3):
        value = jnp.zeros((40, 128), jnp.int32)
        for index in range(4):
            p = (2 * (1 - core) if index < 2 else 2 * core) + index % 2
            value = jnp.where((row & 3) == index, mom_ref[p, axis], value)
        momentum.append(value)
    fx = wrapped(momentum[0] * (line + 24 * lax.axis_index("zh")), 48).astype(jnp.float32) / 48
    fy = wrapped(momentum[1] * (site - line * LY), 48).astype(jnp.float32) / 48
    fz = wrapped(momentum[2] * zpos, 32).astype(jnp.float32) / 32
    theta = (2.0 * math.pi) * (fx + fy + fz)
    cosines = jnp.cos(theta)
    sines = jnp.sin(theta)
    for tile in range(TILES):
        out_ref[tile, :4] = cosines[4 * tile:4 * tile + 4]
        out_ref[tile, 4:] = sines[4 * tile:4 * tile + 4]


def split(value):
    high = value.astype(jnp.bfloat16)
    return high, (value - high.astype(jnp.float32)).astype(jnp.bfloat16)


def build_right(keep_ref, came_ref, halo_ref, halo_came_ref, zkeep_ref, zcame_ref, link_ref, right_ref):
    lane = lax.broadcasted_iota(jnp.int32, (48, 128), 1)

    def load(first_ref, second_ref, reim, tile, color):
        row = reim * 648 + tile * 72 + color * 24
        return jnp.concatenate([first_ref[row:row + 24], second_ref[row:row + 24]], axis=0)

    def beyond_x(reim, tile, color):
        here = pltpu.roll(load(keep_ref, came_ref, reim, tile, color), 80, 1)
        if tile + 1 < TILES:
            after = pltpu.roll(load(keep_ref, came_ref, reim, tile + 1, color), 80, 1)
        else:
            field = reim * 3 + color
            row = field // 2 * 24
            after = jnp.concatenate([halo_ref[row:row + 24], halo_came_ref[row:row + 24]], axis=0)
            after = pltpu.roll(after, 80 - LY * (field % 2), 1)
        return jnp.where(lane < 80, here, after)

    def beyond_y(reim, tile, color):
        here = load(keep_ref, came_ref, reim, tile, color)
        value = pltpu.roll(here, 127, 1)
        back = pltpu.roll(here, 47, 1)
        for at in range(128):
            if (tile * 128 + at) % LY == LY - 1:
                if at >= 47:
                    value = jnp.where(lane == at, back, value)
                else:
                    before = pltpu.roll(load(keep_ref, came_ref, reim, tile - 1, color), 47, 1)
                    value = jnp.where(lane == at, before, value)
        if (tile * 128 + 127) % LY != LY - 1:
            after = pltpu.roll(load(keep_ref, came_ref, reim, tile + 1, color), 127, 1)
            value = jnp.where(lane == 127, after, value)
        return value

    def beyond_z(reim, tile, color):
        return load(zkeep_ref, zcame_ref, reim, tile, color)

    def put(reim, k, tile, color, value):
        row = reim * 192 + k * 48
        column = (tile * 3 + color) * 128
        high, low = split(value)
        right_ref[row:row + 48, column:column + 128] = high
        right_ref[384 + row:384 + row + 48, column:column + 128] = low

    for tile in range(TILES):
        for color in range(3):
            for reim in range(2):
                put(reim, 0, tile, color, load(keep_ref, came_ref, reim, tile, color))
        for direction, beyond in enumerate((beyond_x, beyond_y, beyond_z)):
            far = [[beyond(reim, tile, color) for color in range(3)] for reim in range(2)]
            for row in range(3):
                re = None
                im = None
                for column in range(3):
                    at = direction * 18 + row * 3 + column
                    ur = link_ref[tile, at:at + 1, :]
                    ui = link_ref[tile, at + 9:at + 10, :]
                    more_re = ur * far[0][column] - ui * far[1][column]
                    more_im = ur * far[1][column] + ui * far[0][column]
                    re = more_re if re is None else re + more_re
                    im = more_im if im is None else im + more_im
                put(0, direction + 1, tile, row, re)
                put(1, direction + 1, tile, row, im)


def multiply(blocks, phase_ref, right_ref, away_ref, stay_ref, high_ref, low_ref):
    count = len(blocks)
    rows = 24 * count

    def make_left(tile, carry):
        real = []
        imag = []
        for block in blocks:
            if len(block) == 1:
                real.append(block[0][pl.ds(pl.multiple_of(tile * 72, 8), 72)])
                imag.append(block[0][pl.ds(pl.multiple_of(tile * 72 + 648, 8), 72)])
            else:
                real.append(block[0][pl.ds(pl.multiple_of(tile * 72, 8), 72)])
                imag.append(block[1][pl.ds(pl.multiple_of(tile * 72, 8), 72)])
        for index in range(4):
            cosv = phase_ref[tile, index:index + 1, :]
            sinv = phase_ref[tile, 4 + index:5 + index, :]
            left_real = [a * cosv - b * sinv for a, b in zip(real, imag)]
            left_imag = [-(a * sinv + b * cosv) for a, b in zip(real, imag)]
            for color in range(3):
                value = jnp.concatenate(
                    [part[color * 24:color * 24 + 24] for part in left_real + left_imag], axis=0
                )
                high, low = split(value)
                column = pl.ds(pl.multiple_of(tile * 384 + color * 128, 128), 128)
                high_ref[2 * rows * index:2 * rows * (index + 1), column] = high
                low_ref[2 * rows * index:2 * rows * (index + 1), column] = low
        return carry

    lax.fori_loop(0, TILES, make_left, 0)

    def times(left, right):
        return lax.dot_general(
            left, right, (((1,), (1,)), ((), ())), preferred_element_type=jnp.float32
        )

    both = times(high_ref[...], right_ref[...])
    total = both[:, :384] + both[:, 384:] + times(low_ref[...], right_ref[:384])
    for index in range(4):
        out_ref = (away_ref, stay_ref)[index // 2]
        base = 2 * rows * index
        top = total[base:base + rows]
        low = total[base + rows:base + 2 * rows]
        product = (top[:, :192] - low[:, 192:], low[:, :192] + top[:, 192:])
        for reim in range(2):
            column = (2 * (index % 2) + reim) * 192
            for sub in range(count):
                out_ref[sub, :, column:column + 192] = product[reim][sub * 24:sub * 24 + 24]


def own_kernel(keep, came, halo, halo_came, zkeep, zcame, link, phase, right, away, stay, high, low):
    build_right(keep, came, halo, halo_came, zkeep, zcame, link, right)
    multiply([(keep,), (came,)], phase, right, away, stay, high, low)


def kept_kernel(after, before, far_real, far_imag, phase, right, away, stay, high, low):
    multiply([(after,), (before,), (far_real, far_imag)], phase, right, away, stay, high, low)


def came_kernel(after, before, phase, right, away, stay, high, low):
    multiply([(after,), (before,)], phase, right, away, stay, high, low)


def far_kernel(far_real, far_imag, phase, right, away, stay, high, low):
    multiply([(far_real, far_imag)], phase, right, away, stay, high, low)


def add_kernel(*refs):
    x = lax.axis_index("x")
    zh = lax.axis_index("zh")
    out_ref = refs[8]
    order = (((0, 0), (0, 1)), ((1, 0), (3, 0), (2, 0)), ((1, 1), (3, 1)), ((2, 1),))
    for call_at, blocks in enumerate(order):
        for sub, (distance, came) in enumerate(blocks):
            to = lax.rem(x + distance, 4)
            half = 1 - zh if came else zh
            out_ref[to, pl.ds(pl.multiple_of(half * 24, 8), 24)] = (
                refs[2 * call_at][sub] + refs[2 * call_at + 1][sub]
            )


def pack_kernel(part_ref, out_ref):
    zh = lax.axis_index("zh")
    total = part_ref[0] + part_ref[1] + part_ref[2] + part_ref[3]
    for came in range(2):
        pieces = []
        for piece in range(16):
            begin = piece * 48 + came * 24
            pieces.append(total[:, begin:begin + 24])
        packed = jnp.concatenate(pieces, axis=1)
        half = 1 - zh if came else zh
        for zl in range(4):
            for core in range(2):
                begin = zl * 12 + core * 6
                to = zl * 4 + half * 2 + core
                out_ref[to, :6] = packed[begin:begin + 6]
                out_ref[to, 6:] = jnp.zeros((2, 384), jnp.float32)


def last_kernel(direction_ref, part_ref, out_ref):
    for core in range(2):
        total = part_ref[core]
        for source in range(1, 8):
            total = total + part_ref[2 * source + core]
        total = total[:6]
        for p in range(2):
            for reim in range(2):
                begin = p * 192 + reim * 96
                fields = [total[:, begin + 24 * k:begin + 24 * k + 24] for k in range(4)]
                out_ref[2 * core + p, 0, reim] = fields[0]
                for d in range(1, 4):
                    k = direction_ref[d - 1]
                    value = jnp.where(k == 1, fields[2], fields[1])
                    out_ref[2 * core + p, d, reim] = jnp.where(k == 2, fields[3], value)


def vmem(count):
    return [pl.BlockSpec(memory_space=pltpu.VMEM)] * count


def call(kernel, name, outs, operands, scratch=(), scalars=0):
    out_shape = tuple(
        jax.ShapeDtypeStruct(shape, jnp.bfloat16 if shape == (768, DEPTH) else jnp.float32) for shape in outs
    )
    return pl.pallas_call(
        kernel,
        out_shape=out_shape,
        in_specs=[pl.BlockSpec(memory_space=pltpu.SMEM)] * scalars + vmem(len(operands) - scalars),
        out_specs=tuple(vmem(len(outs))),
        scratch_shapes=list(scratch),
        compiler_params=pltpu.CompilerParams(vmem_limit_bytes=VMEM_BYTES),
        name=name,
    )(*operands)


def along(value, axis, step):
    count = lax.axis_size(axis)
    return lax.ppermute(value, axis, [(i, (i + step) % count) for i in range(count)])


def left_scratch(count):
    return [pltpu.VMEM((192 * count, DEPTH), jnp.bfloat16)] * 2


def local(eigvecs, links, momenta, directions):
    flat = (ROWS, 128)
    keep, send, halo, halo_send, link = call(
        cut_kernel, "cut", [flat, flat, (72, 128), (72, 128), (TILES, 56, 128)],
        (eigvecs.reshape(144, 2304), links.reshape(54, 2304)),
    )
    came = along(send, "zh", 1)
    halo_came = along(halo_send, "zh", 1)
    keep_after = along(keep, "x", -1)
    keep_before = along(keep, "x", 1)
    zkeep = along(keep, SITE, -1)
    phase, = call(phase_kernel, "phase", [(TILES, 8, 128)], (momenta,), (), 1)
    keep_far = (along(keep_after[:648], "x", -1), along(keep_before[648:], "x", 1))
    zcame = along(came, SITE, -1)
    came_after = along(came, "x", -1)
    came_before = along(came, "x", 1)
    came_far = (along(came_after[:648], "x", -1), along(came_before[648:], "x", 1))

    def parts(count):
        return [(count, 24, 768)] * 2

    right, away, stay = call(
        own_kernel, "own", [(768, DEPTH)] + parts(2),
        (keep, came, halo, halo_came, zkeep, zcame, link, phase), left_scratch(2),
    )
    products = [(away, stay)]
    products.append(call(
        kept_kernel, "kept", parts(3), (keep_after, keep_before, *keep_far, phase, right), left_scratch(3)
    ))
    products.append(call(
        came_kernel, "came", parts(2), (came_after, came_before, phase, right), left_scratch(2)
    ))
    products.append(call(far_kernel, "far", parts(1), (*came_far, phase, right), left_scratch(1)))
    terms = []
    for away, stay in products:
        terms += [stay, along(away, "core", 1)]
    ready, = call(add_kernel, "add", [(4, 48, 768)], terms)
    packed, = call(pack_kernel, "pack", [(16, 8, 384)], (lax.all_to_all(ready, "y", 0, 0),))
    mixed = lax.all_to_all(packed, ("zl", "zh", "core"), 0, 0)
    return call(last_kernel, "last", [(4, 4, 2, 6, 24)], (directions, mixed), (), 1)[0]


def solution(mesh):
    fine = Mesh(mesh.devices.reshape(4, 4, 2, 4, 2), ("y", "zl", "core", "x", "zh"))
    ev = ("x", "zh")
    in_specs = (P(None, None, ev, SITE, None), P(None, None, None, None, SITE, None), P(), P())
    out_specs = P(None, None, None, SITE, ev)
    return jax.shard_map(local, mesh=fine, in_specs=in_specs, out_specs=out_specs, check_vma=False)
```

```python
import math

import jax
import jax.numpy as jnp
from jax import lax
from jax.experimental import pallas as pl
from jax.experimental.pallas import tpu as pltpu
from jax.sharding import Mesh
from jax.sharding import PartitionSpec as P

LY = 48
HALF = 1152
TILES = 9
ROWS = 1296
DEPTH = 3456
SITE = ("y", "zl", "core")
VMEM_BYTES = 44 * 1024 * 1024


def cut_kernel(vec_ref, link_ref, keep_ref, send_ref, halo_ref, link_out_ref):
    zh = lax.axis_index("zh")
    for out_ref, other_ref, begin in ((keep_ref, send_ref.at[ROWS:], zh), (send_ref, halo_ref, 1 - zh)):
        for tile in range(TILES):
            at = pl.ds(pl.multiple_of(begin * HALF + tile * 128, 128), 128)
            for reim in range(2):
                row = reim * 648 + tile * 72
                out_ref[row:row + 72] = vec_ref[reim * 72:reim * 72 + 72, at]
        lane = lax.broadcasted_iota(jnp.int32, (24, 128), 1)
        at = pl.ds(pl.multiple_of(begin * HALF, 128), 128)
        for pair in range(3):
            even = vec_ref[pair * 48:pair * 48 + 24, at]
            odd = vec_ref[pair * 48 + 24:pair * 48 + 48, at]
            other_ref[pair * 24:pair * 24 + 24] = jnp.where(lane < LY, even, pltpu.roll(odd, LY, 1))
    for tile in range(TILES):
        at = pl.ds(pl.multiple_of(zh * HALF + tile * 128, 128), 128)
        link_out_ref[tile, :54] = link_ref[:, at]


def wrapped(value, period):
    rest = lax.rem(value, period)
    return jnp.where(rest < 0, rest + period, rest)


def phase_kernel(mom_ref, out_ref):
    core = lax.axis_index("core")
    zpos = lax.axis_index("y") * 8 + lax.axis_index("zl") * 2 + core
    row = lax.broadcasted_iota(jnp.int32, (40, 128), 0)
    site = lax.broadcasted_iota(jnp.int32, (40, 128), 1) + 128 * (row >> 2)
    line = jnp.floor((site.astype(jnp.float32) + 0.5) * (1.0 / LY)).astype(jnp.int32)
    momentum = []
    for axis in range(3):
        value = jnp.zeros((40, 128), jnp.int32)
        for index in range(4):
            p = (2 * (1 - core) if index < 2 else 2 * core) + index % 2
            value = jnp.where((row & 3) == index, mom_ref[p, axis], value)
        momentum.append(value)
    fx = wrapped(momentum[0] * (line + 24 * lax.axis_index("zh")), 48).astype(jnp.float32) / 48
    fy = wrapped(momentum[1] * (site - line * LY), 48).astype(jnp.float32) / 48
    fz = wrapped(momentum[2] * zpos, 32).astype(jnp.float32) / 32
    theta = (2.0 * math.pi) * (fx + fy + fz)
    cosines = jnp.cos(theta)
    sines = jnp.sin(theta)
    for tile in range(TILES):
        out_ref[tile, :4] = cosines[4 * tile:4 * tile + 4]
        out_ref[tile, 4:] = sines[4 * tile:4 * tile + 4]


def split(value):
    high = value.astype(jnp.bfloat16)
    return high, (value - high.astype(jnp.float32)).astype(jnp.bfloat16)


def build_right(keep_ref, came_ref, halo_ref, zkeep_ref, zcame_ref, link_ref, right_ref):
    lane = lax.broadcasted_iota(jnp.int32, (48, 128), 1)

    def load(first_ref, second_ref, reim, tile, color):
        row = reim * 648 + tile * 72 + color * 24
        return jnp.concatenate([first_ref[row:row + 24], second_ref[row:row + 24]], axis=0)

    def beyond_x(reim, tile, color):
        here = pltpu.roll(load(keep_ref, came_ref, reim, tile, color), 80, 1)
        if tile + 1 < TILES:
            after = pltpu.roll(load(keep_ref, came_ref, reim, tile + 1, color), 80, 1)
        else:
            field = reim * 3 + color
            row = field // 2 * 24
            at = ROWS + row
            after = jnp.concatenate([halo_ref[row:row + 24], came_ref[at:at + 24]], axis=0)
            after = pltpu.roll(after, 80 - LY * (field % 2), 1)
        return jnp.where(lane < 80, here, after)

    def beyond_y(reim, tile, color):
        here = load(keep_ref, came_ref, reim, tile, color)
        value = pltpu.roll(here, 127, 1)
        back = pltpu.roll(here, 47, 1)
        for at in range(128):
            if (tile * 128 + at) % LY == LY - 1:
                if at >= 47:
                    value = jnp.where(lane == at, back, value)
                else:
                    before = pltpu.roll(load(keep_ref, came_ref, reim, tile - 1, color), 47, 1)
                    value = jnp.where(lane == at, before, value)
        if (tile * 128 + 127) % LY != LY - 1:
            after = pltpu.roll(load(keep_ref, came_ref, reim, tile + 1, color), 127, 1)
            value = jnp.where(lane == 127, after, value)
        return value

    def beyond_z(reim, tile, color):
        return load(zkeep_ref, zcame_ref, reim, tile, color)

    def put(reim, k, tile, color, value):
        row = reim * 192 + k * 48
        column = (tile * 3 + color) * 128
        high, low = split(value)
        right_ref[row:row + 48, column:column + 128] = high
        right_ref[384 + row:384 + row + 48, column:column + 128] = low

    def build(tile):
        for color in range(3):
            for reim in range(2):
                put(reim, 0, tile, color, load(keep_ref, came_ref, reim, tile, color))
        for direction, beyond in enumerate((beyond_x, beyond_y, beyond_z)):
            far = [[beyond(reim, tile, color) for color in range(3)] for reim in range(2)]
            for row in range(3):
                re = None
                im = None
                for column in range(3):
                    at = direction * 18 + row * 3 + column
                    ur = link_ref[tile, at:at + 1, :]
                    ui = link_ref[tile, at + 9:at + 10, :]
                    more_re = ur * far[0][column] - ui * far[1][column]
                    more_im = ur * far[1][column] + ui * far[0][column]
                    re = more_re if re is None else re + more_re
                    im = more_im if im is None else im + more_im
                put(0, direction + 1, tile, row, re)
                put(1, direction + 1, tile, row, im)

    return build


def multiply(blocks, phase_ref, right_ref, away_ref, stay_ref, high_ref, low_ref, build=None):
    count = len(blocks)
    rows = 24 * count

    def make_left(tile):
        for index in range(4):
            cosv = phase_ref[tile, index:index + 1, :]
            sinv = phase_ref[tile, 4 + index:5 + index, :]
            for color in range(3):
                row = tile * 72 + color * 24
                left_real = []
                left_imag = []
                for block in blocks:
                    a = block[row:row + 24]
                    b = block[row + 648:row + 672]
                    left_real.append(a * cosv - b * sinv)
                    left_imag.append(-(a * sinv + b * cosv))
                high, low = split(jnp.concatenate(left_real + left_imag, axis=0))
                column = tile * 384 + color * 128
                high_ref[2 * rows * index:2 * rows * (index + 1), column:column + 128] = high
                low_ref[2 * rows * index:2 * rows * (index + 1), column:column + 128] = low

    def prepare(chunk):
        for tile in range(3 * chunk, 3 * chunk + 3):
            if build is not None:
                build(tile)
            make_left(tile)

    def times(left, right):
        return lax.dot_general(
            left, right, (((1,), (1,)), ((), ())), preferred_element_type=jnp.float32
        )

    prepare(0)
    total = None
    for chunk in range(3):
        if chunk < 2:
            prepare(chunk + 1)
        part = slice(chunk * HALF, (chunk + 1) * HALF)
        both = times(high_ref[:, part], right_ref[:, part])
        more = both[:, :384] + both[:, 384:] + times(low_ref[:, part], right_ref[:384, part])
        total = more if total is None else total + more
    for index in range(4):
        out_ref = (away_ref, stay_ref)[index // 2]
        base = 2 * rows * index
        top = total[base:base + rows]
        low = total[base + rows:base + 2 * rows]
        product = (top[:, :192] - low[:, 192:], low[:, :192] + top[:, 192:])
        for reim in range(2):
            column = (2 * (index % 2) + reim) * 192
            for sub in range(count):
                out_ref[sub, :, column:column + 192] = product[reim][sub * 24:sub * 24 + 24]


def own_kernel(keep, came, halo, zkeep, zcame, link, phase, right, away, stay, high, low):
    build = build_right(keep, came, halo, zkeep, zcame, link, right)
    multiply([keep, came], phase, right, away, stay, high, low, build)


def kept_kernel(after, before, far, phase, right, away, stay, high, low):
    multiply([after, before, far], phase, right, away, stay, high, low)


def came_kernel(after, before, phase, right, away, stay, high, low):
    multiply([after, before], phase, right, away, stay, high, low)


def far_kernel(far, phase, right, away, stay, high, low):
    multiply([far], phase, right, away, stay, high, low)


def add_kernel(*refs):
    x = lax.axis_index("x")
    zh = lax.axis_index("zh")
    out_ref = refs[8]
    order = (((0, 0), (0, 1)), ((1, 0), (3, 0), (2, 0)), ((1, 1), (3, 1)), ((2, 1),))
    for call_at, blocks in enumerate(order):
        for sub, (distance, came) in enumerate(blocks):
            to = lax.rem(x + distance, 4)
            half = 1 - zh if came else zh
            out_ref[to, pl.ds(pl.multiple_of(half * 24, 8), 24)] = (
                refs[2 * call_at][sub] + refs[2 * call_at + 1][sub]
            )


def pack_kernel(part_ref, out_ref):
    zh = lax.axis_index("zh")
    total = part_ref[0] + part_ref[1] + part_ref[2] + part_ref[3]
    for came in range(2):
        pieces = []
        for piece in range(16):
            begin = piece * 48 + came * 24
            pieces.append(total[:, begin:begin + 24])
        packed = jnp.concatenate(pieces, axis=1)
        half = 1 - zh if came else zh
        for zl in range(4):
            for core in range(2):
                begin = zl * 12 + core * 6
                to = zl * 4 + half * 2 + core
                out_ref[to, :6] = packed[begin:begin + 6]
                out_ref[to, 6:] = jnp.zeros((2, 384), jnp.float32)


def last_kernel(direction_ref, part_ref, out_ref):
    for core in range(2):
        total = part_ref[core]
        for source in range(1, 8):
            total = total + part_ref[2 * source + core]
        total = total[:6]
        for p in range(2):
            for reim in range(2):
                begin = p * 192 + reim * 96
                fields = [total[:, begin + 24 * k:begin + 24 * k + 24] for k in range(4)]
                out_ref[2 * core + p, 0, reim] = fields[0]
                for d in range(1, 4):
                    k = direction_ref[d - 1]
                    value = jnp.where(k == 1, fields[2], fields[1])
                    out_ref[2 * core + p, d, reim] = jnp.where(k == 2, fields[3], value)


def vmem(count):
    return [pl.BlockSpec(memory_space=pltpu.VMEM)] * count


def call(kernel, name, outs, operands, scratch=(), scalars=0, micros=1):
    out_shape = tuple(
        jax.ShapeDtypeStruct(shape, jnp.bfloat16 if shape == (768, DEPTH) else jnp.float32) for shape in outs
    )
    return pl.pallas_call(
        kernel,
        out_shape=out_shape,
        in_specs=[pl.BlockSpec(memory_space=pltpu.SMEM)] * scalars + vmem(len(operands) - scalars),
        out_specs=tuple(vmem(len(outs))),
        scratch_shapes=list(scratch),
        compiler_params=pltpu.CompilerParams(vmem_limit_bytes=VMEM_BYTES),
        cost_estimate=pl.CostEstimate(
            flops=int(micros * 0.3e9), bytes_accessed=int(micros * 0.3 * 3.0e6), transcendentals=0
        ),
        name=name,
    )(*operands)


def along(value, axis, step):
    count = lax.axis_size(axis)
    return lax.ppermute(value, axis, [(i, (i + step) % count) for i in range(count)])


def left_scratch(count):
    return [pltpu.VMEM((192 * count, DEPTH), jnp.bfloat16)] * 2


def local(eigvecs, links, momenta, directions):
    flat = (ROWS, 128)
    keep, send, halo, link = call(
        cut_kernel, "cut", [flat, (ROWS + 72, 128), (72, 128), (TILES, 56, 128)],
        (eigvecs.reshape(144, 2304), links.reshape(54, 2304)),
    )
    came = along(send, "zh", 1)
    keep_after = along(keep, "x", -1)
    keep_before = along(keep, "x", 1)
    zkeep = along(keep, SITE, -1)
    phase, = call(phase_kernel, "phase", [(TILES, 8, 128)], (momenta,), (), 1)
    keep_far = along(keep, "x", 2)
    came, keep_after, keep_before, keep_far = lax.optimization_barrier((came, keep_after, keep_before, keep_far))
    zcame = along(came, SITE, -1)
    came_after = along(came, "x", -1)
    came_before = along(came, "x", 1)
    came_far = along(came, "x", 2)

    def parts(count):
        return [(count, 24, 768)] * 2

    right, away, stay = call(
        own_kernel, "own", [(768, DEPTH)] + parts(2),
        (keep, came, halo, zkeep, zcame, link, phase), left_scratch(2), 0, 9,
    )
    products = [(away, stay)]
    products.append(call(
        kept_kernel, "kept", parts(3), (keep_after, keep_before, keep_far, phase, right), left_scratch(3), 0, 8
    ))
    products.append(call(
        came_kernel, "came", parts(2), (came_after, came_before, phase, right), left_scratch(2), 0, 6
    ))
    products.append(call(far_kernel, "far", parts(1), (came_far, phase, right), left_scratch(1), 0, 4))
    terms = []
    for away, stay in products:
        terms += [stay, along(away, "core", 1)]
    ready, = call(add_kernel, "add", [(4, 48, 768)], terms)
    packed, = call(pack_kernel, "pack", [(16, 8, 384)], (lax.all_to_all(ready, "y", 0, 0),))
    mixed = lax.all_to_all(packed, ("zl", "zh", "core"), 0, 0)
    return call(last_kernel, "last", [(4, 4, 2, 6, 24)], (directions, mixed), (), 1)[0]


def solution(mesh):
    fine = Mesh(mesh.devices.reshape(4, 4, 2, 4, 2), ("y", "zl", "core", "x", "zh"))
    ev = ("x", "zh")
    in_specs = (P(None, None, ev, SITE, None), P(None, None, None, None, SITE, None), P(), P())
    out_specs = P(None, None, None, SITE, ev)
    return jax.shard_map(local, mesh=fine, in_specs=in_specs, out_specs=out_specs, check_vma=False)
```

```python
import math

import jax
import jax.numpy as jnp
from jax import lax
from jax.experimental import pallas as pl
from jax.experimental.pallas import tpu as pltpu
from jax.sharding import Mesh
from jax.sharding import PartitionSpec as P

LY = 48
HALF = 1152
TILES = 9
ROWS = 1296
DEPTH = 3456
SITE = ("y", "zl", "core")
VMEM_BYTES = 44 * 1024 * 1024


def cut_kernel(vec_ref, keep_ref, send_ref, halo_ref):
    zh = lax.axis_index("zh")
    for out_ref, other_ref, begin in ((keep_ref, send_ref.at[ROWS:], zh), (send_ref, halo_ref, 1 - zh)):
        for tile in range(TILES):
            at = pl.ds(pl.multiple_of(begin * HALF + tile * 128, 128), 128)
            for reim in range(2):
                row = reim * 648 + tile * 72
                out_ref[row:row + 72] = vec_ref[reim * 72:reim * 72 + 72, at]
        lane = lax.broadcasted_iota(jnp.int32, (24, 128), 1)
        at = pl.ds(pl.multiple_of(begin * HALF, 128), 128)
        for pair in range(3):
            even = vec_ref[pair * 48:pair * 48 + 24, at]
            odd = vec_ref[pair * 48 + 24:pair * 48 + 48, at]
            other_ref[pair * 24:pair * 24 + 24] = jnp.where(lane < LY, even, pltpu.roll(odd, LY, 1))

def link_kernel(link_ref, out_ref):
    zh = lax.axis_index("zh")
    for tile in range(TILES):
        at = pl.ds(pl.multiple_of(zh * HALF + tile * 128, 128), 128)
        out_ref[tile, :54] = link_ref[:, at]


def wrapped(value, period):
    rest = lax.rem(value, period)
    return jnp.where(rest < 0, rest + period, rest)


def phase_kernel(mom_ref, out_ref):
    core = lax.axis_index("core")
    zpos = lax.axis_index("y") * 8 + lax.axis_index("zl") * 2 + core
    row = lax.broadcasted_iota(jnp.int32, (40, 128), 0)
    site = lax.broadcasted_iota(jnp.int32, (40, 128), 1) + 128 * (row >> 2)
    line = jnp.floor((site.astype(jnp.float32) + 0.5) * (1.0 / LY)).astype(jnp.int32)
    momentum = []
    for axis in range(3):
        value = jnp.zeros((40, 128), jnp.int32)
        for index in range(4):
            p = (2 * (1 - core) if index < 2 else 2 * core) + index % 2
            value = jnp.where((row & 3) == index, mom_ref[p, axis], value)
        momentum.append(value)
    fx = wrapped(momentum[0] * (line + 24 * lax.axis_index("zh")), 48).astype(jnp.float32) / 48
    fy = wrapped(momentum[1] * (site - line * LY), 48).astype(jnp.float32) / 48
    fz = wrapped(momentum[2] * zpos, 32).astype(jnp.float32) / 32
    theta = (2.0 * math.pi) * (fx + fy + fz)
    cosines = jnp.cos(theta)
    sines = jnp.sin(theta)
    for tile in range(TILES):
        out_ref[tile, :4] = cosines[4 * tile:4 * tile + 4]
        out_ref[tile, 4:] = sines[4 * tile:4 * tile + 4]


def split(value):
    high = value.astype(jnp.bfloat16)
    return high, (value - high.astype(jnp.float32)).astype(jnp.bfloat16)


def load(first_ref, second_ref, reim, tile, color):
    row = reim * 648 + tile * 72 + color * 24
    return jnp.concatenate([first_ref[row:row + 24], second_ref[row:row + 24]], axis=0)


def put(right_ref, fields, reim, k, tile, color, value):
    row = (reim * fields + k) * 48
    column = (tile * 3 + color) * 128
    high, low = split(value)
    right_ref[row:row + 48, column:column + 128] = high
    right_ref[96 * fields + row:96 * fields + row + 48, column:column + 128] = low


def transport(right_ref, fields, k, tile, far, link_ref, direction):
    for row in range(3):
        re = None
        im = None
        for column in range(3):
            at = direction * 18 + row * 3 + column
            ur = link_ref[tile, at:at + 1, :]
            ui = link_ref[tile, at + 9:at + 10, :]
            more_re = ur * far[0][column] - ui * far[1][column]
            more_im = ur * far[1][column] + ui * far[0][column]
            re = more_re if re is None else re + more_re
            im = more_im if im is None else im + more_im
        put(right_ref, fields, 0, k, tile, row, re)
        put(right_ref, fields, 1, k, tile, row, im)


def build_plane(keep_ref, came_ref, halo_ref, link_ref, right_ref):
    lane = lax.broadcasted_iota(jnp.int32, (48, 128), 1)

    def beyond_x(reim, tile, color):
        here = pltpu.roll(load(keep_ref, came_ref, reim, tile, color), 80, 1)
        if tile + 1 < TILES:
            after = pltpu.roll(load(keep_ref, came_ref, reim, tile + 1, color), 80, 1)
        else:
            field = reim * 3 + color
            row = field // 2 * 24
            at = ROWS + row
            after = jnp.concatenate([halo_ref[row:row + 24], came_ref[at:at + 24]], axis=0)
            after = pltpu.roll(after, 80 - LY * (field % 2), 1)
        return jnp.where(lane < 80, here, after)

    def beyond_y(reim, tile, color):
        here = load(keep_ref, came_ref, reim, tile, color)
        value = pltpu.roll(here, 127, 1)
        back = pltpu.roll(here, 47, 1)
        for at in range(128):
            if (tile * 128 + at) % LY == LY - 1:
                if at >= 47:
                    value = jnp.where(lane == at, back, value)
                else:
                    before = pltpu.roll(load(keep_ref, came_ref, reim, tile - 1, color), 47, 1)
                    value = jnp.where(lane == at, before, value)
        if (tile * 128 + 127) % LY != LY - 1:
            after = pltpu.roll(load(keep_ref, came_ref, reim, tile + 1, color), 127, 1)
            value = jnp.where(lane == 127, after, value)
        return value

    def build(tile):
        for color in range(3):
            for reim in range(2):
                put(right_ref, 3, reim, 0, tile, color, load(keep_ref, came_ref, reim, tile, color))
        for direction, beyond in enumerate((beyond_x, beyond_y)):
            far = [[beyond(reim, tile, color) for color in range(3)] for reim in range(2)]
            transport(right_ref, 3, direction + 1, tile, far, link_ref, direction)

    return build


def build_z(zkeep_ref, zcame_ref, link_ref, right_ref):
    def build(tile):
        far = [[load(zkeep_ref, zcame_ref, reim, tile, color) for color in range(3)] for reim in range(2)]
        transport(right_ref, 1, 0, tile, far, link_ref, 2)

    return build


def multiply(blocks, phase_ref, rights, first, away_ref, stay_ref, high_ref, low_ref, build=None, offset=0):
    count = len(blocks)
    rows = 24 * count

    def make_left(tile):
        for index in range(4):
            cosv = phase_ref[tile, index:index + 1, :]
            sinv = phase_ref[tile, 4 + index:5 + index, :]
            for color in range(3):
                row = tile * 72 + color * 24
                left_real = []
                left_imag = []
                for block in blocks:
                    a = block[row:row + 24]
                    b = block[row + 648:row + 672]
                    left_real.append(a * cosv - b * sinv)
                    left_imag.append(-(a * sinv + b * cosv))
                high, low = split(jnp.concatenate(left_real + left_imag, axis=0))
                column = tile * 384 + color * 128
                high_ref[2 * rows * index:2 * rows * (index + 1), column:column + 128] = high
                low_ref[2 * rows * index:2 * rows * (index + 1), column:column + 128] = low

    def prepare(chunk):
        for tile in range(3 * chunk, 3 * chunk + 3):
            if build is not None:
                build(tile)
            make_left(tile)

    def times(left, right):
        return lax.dot_general(
            left, right, (((1,), (1,)), ((), ())), preferred_element_type=jnp.float32
        )

    def joined(parts):
        return parts[0] if len(parts) == 1 else jnp.concatenate(parts, axis=0)

    widths = [ref.shape[0] // 4 for ref in rights]
    count_high = 2 * sum(widths)
    prepare(0)
    total = None
    for chunk in range(3):
        if chunk < 2:
            prepare(chunk + 1)
        part = slice(chunk * HALF, (chunk + 1) * HALF)
        highs = [ref[:2 * width, part] for ref, width in zip(rights, widths)]
        lows = [ref[2 * width:, part] for ref, width in zip(rights, widths)]
        both = times(high_ref[:, part], joined(highs + lows))
        more = both[:, :count_high] + both[:, count_high:] + times(low_ref[:, part], joined(highs))
        total = more if total is None else total + more
    for index in range(4):
        out_ref = (away_ref, stay_ref)[index // 2]
        base = 2 * rows * index
        top = total[base:base + rows]
        low = total[base + rows:base + 2 * rows]
        begin = 0
        to = first * 48
        for width in widths:
            mid = begin + width
            end = mid + width
            product = (top[:, begin:mid] - low[:, mid:end], low[:, begin:mid] + top[:, mid:end])
            for reim in range(2):
                column = (2 * (index % 2) + reim) * 192 + to
                for sub in range(count):
                    out_ref[offset + sub, :, column:column + width] = product[reim][sub * 24:sub * 24 + 24]
            begin = end
            to += width


def own_kernel(keep, came, halo, link, phase, right, away, stay, high, low):
    build = build_plane(keep, came, halo, link, right)
    multiply([keep, came], phase, (right,), 0, away, stay, high, low, build)


def kept_kernel(after, before, far, zkeep, zcame, link, phase, right, zright, away, stay, high, low):
    build = build_z(zkeep, zcame, link, zright)
    multiply([after, before, far], phase, (right, zright), 0, away, stay, high, low, build)


def forward_kernel(after, before, away, first, second):
    first[...] = after[:648]
    second[...] = before[648:ROWS]


class Halves:
    def __init__(self, real, imag):
        self.parts = (real, imag)

    def __getitem__(self, rows):
        return self.parts[rows.start // 648][rows.start % 648:rows.start % 648 + 24]


def came_kernel(
    keep, came, after, before, own_away, own_stay, phase, right, zright,
    away, stay, own_high, own_low, high, low,
):
    away[:2] = own_away[...]
    stay[:2] = own_stay[...]
    multiply([keep, came], phase, (zright,), 3, away, stay, own_high, own_low)
    multiply([after, before], phase, (right, zright), 0, away, stay, high, low, offset=2)


def far_kernel(real, imag, phase, right, zright, away, stay, high, low):
    multiply([Halves(real, imag)], phase, (right, zright), 0, away, stay, high, low)


def add_kernel(*refs):
    x = lax.axis_index("x")
    y = lax.axis_index("y")
    zh = lax.axis_index("zh")
    outs, held = refs[6:10], refs[10]
    order = (((1, 0), (3, 0), (2, 0)), ((0, 0), (0, 1), (1, 1), (3, 1)), ((2, 1),))
    for call_at, blocks in enumerate(order):
        for sub, (distance, came) in enumerate(blocks):
            to = lax.rem(x + distance - y + 4, 4)
            half = 1 - zh if came else zh
            held[to, pl.ds(pl.multiple_of(half * 24, 8), 24)] = refs[2 * call_at][sub] + refs[2 * call_at + 1][sub]
    for step in range(4):
        outs[step][...] = held[step]


def pack_kernel(first, second, third, fourth, out_ref):
    zh = lax.axis_index("zh")
    total = first[...] + second[...] + third[...] + fourth[...]
    for came in range(2):
        pieces = []
        for piece in range(16):
            begin = piece * 48 + came * 24
            pieces.append(total[:, begin:begin + 24])
        packed = jnp.concatenate(pieces, axis=1)
        half = 1 - zh if came else zh
        for zl in range(4):
            for core in range(2):
                begin = zl * 12 + core * 6
                to = zl * 4 + half * 2 + core
                out_ref[to, :6] = packed[begin:begin + 6]
                out_ref[to, 6:] = jnp.zeros((2, 384), jnp.float32)


def last_kernel(direction_ref, part_ref, out_ref):
    for core in range(2):
        total = part_ref[core]
        for source in range(1, 8):
            total = total + part_ref[2 * source + core]
        total = total[:6]
        for p in range(2):
            for reim in range(2):
                begin = p * 192 + reim * 96
                fields = [total[:, begin + 24 * k:begin + 24 * k + 24] for k in range(4)]
                out_ref[2 * core + p, 0, reim] = fields[0]
                for d in range(1, 4):
                    k = direction_ref[d - 1]
                    value = jnp.where(k == 1, fields[2], fields[1])
                    out_ref[2 * core + p, d, reim] = jnp.where(k == 2, fields[3], value)


def vmem(count):
    return [pl.BlockSpec(memory_space=pltpu.VMEM)] * count


def call(kernel, name, outs, operands, scratch=(), scalars=0, micros=1):
    out_shape = tuple(
        jax.ShapeDtypeStruct(shape, jnp.bfloat16 if shape[-1] == DEPTH else jnp.float32) for shape in outs
    )
    return pl.pallas_call(
        kernel,
        out_shape=out_shape,
        in_specs=[pl.BlockSpec(memory_space=pltpu.SMEM)] * scalars + vmem(len(operands) - scalars),
        out_specs=tuple(vmem(len(outs))),
        scratch_shapes=list(scratch),
        compiler_params=pltpu.CompilerParams(vmem_limit_bytes=VMEM_BYTES),
        cost_estimate=pl.CostEstimate(
            flops=int(micros * 0.3e9), bytes_accessed=int(micros * 0.3 * 3.0e6), transcendentals=0
        ),
        name=name,
    )(*operands)


def along(value, axis, step):
    count = lax.axis_size(axis)
    return lax.ppermute(value, axis, [(i, (i + step) % count) for i in range(count)])


def left_scratch(count):
    return [pltpu.VMEM((192 * count, DEPTH), jnp.bfloat16)] * 2


def local(eigvecs, links, momenta, directions):
    flat = (ROWS, 128)
    keep, send, halo = call(
        cut_kernel, "cut", [flat, (ROWS + 72, 128), (72, 128)], (eigvecs.reshape(144, 2304),)
    )
    came = along(send, "zh", 1)
    keep_after = along(keep, "x", -1)
    keep_before = along(keep, "x", 1)
    zkeep = along(keep, SITE, -1)
    phase, = call(phase_kernel, "phase", [(TILES, 8, 128)], (momenta,), (), 1)
    link, = call(link_kernel, "link", [(TILES, 56, 128)], (links.reshape(54, 2304),))
    later, link, phase = lax.optimization_barrier((keep, link, phase))
    keep_far = along(later, "x", 2)
    came, keep_after, keep_before, keep_far, zkeep = lax.optimization_barrier(
        (came, keep_after, keep_before, keep_far, zkeep)
    )
    zcame = along(came, SITE, -1)
    came_after = along(came, "x", -1)
    came_before = along(came, "x", 1)

    def parts(count):
        return [(count, 24, 768)] * 2

    right, own_away, own_stay = call(
        own_kernel, "own", [(576, DEPTH)] + parts(2), (keep, came, halo, link, phase), left_scratch(2), 0, 6,
    )
    zright, away, stay = call(
        kept_kernel, "kept", [(192, DEPTH)] + parts(3),
        (keep_after, keep_before, keep_far, zkeep, zcame, link, phase, right), left_scratch(3), 0, 6,
    )
    products = [(away, stay)]
    half = (648, 128)
    first, second = call(forward_kernel, "forward", [half, half], (came_after, came_before, away))
    came_far = (along(first, "x", -1), along(second, "x", 1))
    products.append(call(
        came_kernel, "came", parts(4),
        (keep, came, came_after, came_before, own_away, own_stay, phase, right, zright),
        left_scratch(2) * 2, 0, 7,
    ))
    products.append(call(
        far_kernel, "far", parts(1), (*came_far, phase, right, zright), left_scratch(1), 0, 3
    ))
    terms = []
    for away, stay in products:
        terms += [stay, along(away, "core", 1)]
    ready = call(add_kernel, "add", [(48, 768)] * 4, terms, [pltpu.VMEM((4, 48, 768), jnp.float32)])
    sums = [ready[0]] + [along(ready[step], "y", step) for step in range(1, 4)]
    packed, = call(pack_kernel, "pack", [(16, 8, 384)], sums)
    mixed = lax.all_to_all(packed, ("zl", "zh", "core"), 0, 0)
    return call(last_kernel, "last", [(4, 4, 2, 6, 24)], (directions, mixed), (), 1)[0]


def solution(mesh):
    fine = Mesh(mesh.devices.reshape(4, 4, 2, 4, 2), ("y", "zl", "core", "x", "zh"))
    ev = ("x", "zh")
    in_specs = (P(None, None, ev, SITE, None), P(None, None, None, None, SITE, None), P(), P())
    out_specs = P(None, None, None, SITE, ev)
    return jax.shard_map(local, mesh=fine, in_specs=in_specs, out_specs=out_specs, check_vma=False)
```

```python
import math

import jax
import jax.numpy as jnp
from jax import lax
from jax.experimental import pallas as pl
from jax.experimental.pallas import tpu as pltpu
from jax.sharding import Mesh
from jax.sharding import PartitionSpec as P

LY = 48
HALF = 1152
TILES = 9
ROWS = 1296
DEPTH = 3456
SITE = ("y", "zl", "core")
VMEM_BYTES = 26 * 1024 * 1024


def cut_kernel(vec_ref, keep_ref, send_ref, halo_ref):
    zh = lax.axis_index("zh")
    for out_ref, other_ref, begin in ((keep_ref, send_ref.at[ROWS:], zh), (send_ref, halo_ref, 1 - zh)):
        for tile in range(TILES):
            at = pl.ds(pl.multiple_of(begin * HALF + tile * 128, 128), 128)
            for reim in range(2):
                row = reim * 648 + tile * 72
                out_ref[row:row + 72] = vec_ref[reim * 72:reim * 72 + 72, at]
        lane = lax.broadcasted_iota(jnp.int32, (24, 128), 1)
        at = pl.ds(pl.multiple_of(begin * HALF, 128), 128)
        for pair in range(3):
            even = vec_ref[pair * 48:pair * 48 + 24, at]
            odd = vec_ref[pair * 48 + 24:pair * 48 + 48, at]
            other_ref[pair * 24:pair * 24 + 24] = jnp.where(lane < LY, even, pltpu.roll(odd, LY, 1))

def link_kernel(link_ref, out_ref):
    zh = lax.axis_index("zh")
    for tile in range(TILES):
        at = pl.ds(pl.multiple_of(zh * HALF + tile * 128, 128), 128)
        out_ref[tile, :54] = link_ref[:, at]


def wrapped(value, period):
    rest = lax.rem(value, period)
    return jnp.where(rest < 0, rest + period, rest)


def phase_kernel(mom_ref, out_ref):
    core = lax.axis_index("core")
    zpos = lax.axis_index("y") * 8 + lax.axis_index("zl") * 2 + core
    row = lax.broadcasted_iota(jnp.int32, (40, 128), 0)
    site = lax.broadcasted_iota(jnp.int32, (40, 128), 1) + 128 * (row >> 2)
    line = jnp.floor((site.astype(jnp.float32) + 0.5) * (1.0 / LY)).astype(jnp.int32)
    momentum = []
    for axis in range(3):
        value = jnp.zeros((40, 128), jnp.int32)
        for index in range(4):
            p = (2 * (1 - core) if index < 2 else 2 * core) + index % 2
            value = jnp.where((row & 3) == index, mom_ref[p, axis], value)
        momentum.append(value)
    fx = wrapped(momentum[0] * (line + 24 * lax.axis_index("zh")), 48).astype(jnp.float32) / 48
    fy = wrapped(momentum[1] * (site - line * LY), 48).astype(jnp.float32) / 48
    fz = wrapped(momentum[2] * zpos, 32).astype(jnp.float32) / 32
    theta = (2.0 * math.pi) * (fx + fy + fz)
    cosines = jnp.cos(theta)
    sines = jnp.sin(theta)
    for tile in range(TILES):
        out_ref[tile, :4] = cosines[4 * tile:4 * tile + 4]
        out_ref[tile, 4:] = sines[4 * tile:4 * tile + 4]


def split(value):
    high = value.astype(jnp.bfloat16)
    return high, (value - high.astype(jnp.float32)).astype(jnp.bfloat16)


def load(first_ref, second_ref, reim, tile, color):
    row = reim * 648 + tile * 72 + color * 24
    return jnp.concatenate([first_ref[row:row + 24], second_ref[row:row + 24]], axis=0)


def put(right_ref, fields, reim, k, tile, color, value):
    row = (reim * fields + k) * 48
    column = (tile * 3 + color) * 128
    high, low = split(value)
    right_ref[row:row + 48, column:column + 128] = high
    right_ref[96 * fields + row:96 * fields + row + 48, column:column + 128] = low


def transport(right_ref, fields, k, tile, far, link_ref, direction):
    for row in range(3):
        re = None
        im = None
        for column in range(3):
            at = direction * 18 + row * 3 + column
            ur = link_ref[tile, at:at + 1, :]
            ui = link_ref[tile, at + 9:at + 10, :]
            more_re = ur * far[0][column] - ui * far[1][column]
            more_im = ur * far[1][column] + ui * far[0][column]
            re = more_re if re is None else re + more_re
            im = more_im if im is None else im + more_im
        put(right_ref, fields, 0, k, tile, row, re)
        put(right_ref, fields, 1, k, tile, row, im)


def build_plane(keep_ref, came_ref, halo_ref, link_ref, right_ref):
    lane = lax.broadcasted_iota(jnp.int32, (48, 128), 1)

    def beyond_x(reim, tile, color):
        here = pltpu.roll(load(keep_ref, came_ref, reim, tile, color), 80, 1)
        if tile + 1 < TILES:
            after = pltpu.roll(load(keep_ref, came_ref, reim, tile + 1, color), 80, 1)
        else:
            field = reim * 3 + color
            row = field // 2 * 24
            at = ROWS + row
            after = jnp.concatenate([halo_ref[row:row + 24], came_ref[at:at + 24]], axis=0)
            after = pltpu.roll(after, 80 - LY * (field % 2), 1)
        return jnp.where(lane < 80, here, after)

    def beyond_y(reim, tile, color):
        here = load(keep_ref, came_ref, reim, tile, color)
        value = pltpu.roll(here, 127, 1)
        back = pltpu.roll(here, 47, 1)
        for at in range(128):
            if (tile * 128 + at) % LY == LY - 1:
                if at >= 47:
                    value = jnp.where(lane == at, back, value)
                else:
                    before = pltpu.roll(load(keep_ref, came_ref, reim, tile - 1, color), 47, 1)
                    value = jnp.where(lane == at, before, value)
        if (tile * 128 + 127) % LY != LY - 1:
            after = pltpu.roll(load(keep_ref, came_ref, reim, tile + 1, color), 127, 1)
            value = jnp.where(lane == 127, after, value)
        return value

    def build(tile):
        for color in range(3):
            for reim in range(2):
                put(right_ref, 3, reim, 0, tile, color, load(keep_ref, came_ref, reim, tile, color))
        for direction, beyond in enumerate((beyond_x, beyond_y)):
            far = [[beyond(reim, tile, color) for color in range(3)] for reim in range(2)]
            transport(right_ref, 3, direction + 1, tile, far, link_ref, direction)

    return build


def build_z(zkeep_ref, zcame_ref, link_ref, right_ref):
    def build(tile):
        far = [[load(zkeep_ref, zcame_ref, reim, tile, color) for color in range(3)] for reim in range(2)]
        transport(right_ref, 1, 0, tile, far, link_ref, 2)

    return build


def multiply(blocks, phase_ref, rights, first, away_ref, stay_ref, high_ref, low_ref, build=None, offset=0):
    count = len(blocks)
    rows = 24 * count

    def make_left(tile):
        for index in range(4):
            cosv = phase_ref[tile, index:index + 1, :]
            sinv = phase_ref[tile, 4 + index:5 + index, :]
            for color in range(3):
                row = tile * 72 + color * 24
                left_real = []
                left_imag = []
                for block in blocks:
                    a = block[row:row + 24]
                    b = block[row + 648:row + 672]
                    left_real.append(a * cosv - b * sinv)
                    left_imag.append(-(a * sinv + b * cosv))
                high, low = split(jnp.concatenate(left_real + left_imag, axis=0))
                column = tile * 384 + color * 128
                high_ref[2 * rows * index:2 * rows * (index + 1), column:column + 128] = high
                low_ref[2 * rows * index:2 * rows * (index + 1), column:column + 128] = low

    def prepare(chunk):
        for tile in range(3 * chunk, 3 * chunk + 3):
            if build is not None:
                build(tile)
            make_left(tile)

    def times(left, right):
        return lax.dot_general(
            left, right, (((1,), (1,)), ((), ())), preferred_element_type=jnp.float32
        )

    def joined(parts):
        return parts[0] if len(parts) == 1 else jnp.concatenate(parts, axis=0)

    widths = [ref.shape[0] // 4 for ref in rights]
    count_high = 2 * sum(widths)
    if blocks[0] is not None:
        prepare(0)
    total = None
    for chunk in range(3):
        if chunk < 2 and blocks[0] is not None:
            prepare(chunk + 1)
        part = slice(chunk * HALF, (chunk + 1) * HALF)
        highs = [ref[:2 * width, part] for ref, width in zip(rights, widths)]
        lows = [ref[2 * width:, part] for ref, width in zip(rights, widths)]
        both = times(high_ref[:, part], joined(highs + lows))
        more = both[:, :count_high] + both[:, count_high:] + times(low_ref[:, part], joined(highs))
        total = more if total is None else total + more
    for index in range(4):
        out_ref = (away_ref, stay_ref)[index // 2]
        base = 2 * rows * index
        top = total[base:base + rows]
        low = total[base + rows:base + 2 * rows]
        begin = 0
        to = first * 48
        for width in widths:
            mid = begin + width
            end = mid + width
            product = (top[:, begin:mid] - low[:, mid:end], low[:, begin:mid] + top[:, mid:end])
            for reim in range(2):
                column = (2 * (index % 2) + reim) * 192 + to
                for sub in range(count):
                    out_ref[offset + sub, :, column:column + width] = product[reim][sub * 24:sub * 24 + 24]
            begin = end
            to += width


def own_kernel(keep, came, halo, link, phase, right, away, stay, high, low):
    build = build_plane(keep, came, halo, link, right)
    multiply([keep, came], phase, (right,), 0, away, stay, high, low, build)


def kept_kernel(after, before, real, imag, phase, right, away, stay, high, low):
    multiply([after, before, Halves(real, imag)], phase, (right,), 0, away, stay, high, low)


def z_kernel(
    own_away, own_stay, own_high, own_low, kept_away, kept_stay, kept_high, kept_low,
    zkeep, zcame, link, zright, away, stay,
):
    away[:2] = own_away[...]
    away[2:] = kept_away[...]
    stay[:2] = own_stay[...]
    stay[2:] = kept_stay[...]
    build = build_z(zkeep, zcame, link, zright)
    for tile in range(TILES):
        build(tile)
    multiply([None] * 2, None, (zright,), 3, away, stay, own_high, own_low)
    multiply([None] * 3, None, (zright,), 3, away, stay, kept_high, kept_low, offset=2)


def forward_kernel(after, before, away, first, second):
    first[...] = after[:648]
    second[...] = before[648:ROWS]


class Halves:
    def __init__(self, real, imag):
        self.parts = (real, imag)

    def __getitem__(self, rows):
        return self.parts[rows.start // 648][rows.start % 648:rows.start % 648 + 24]


def came_kernel(after, before, phase, right, zright, away, stay, high, low):
    multiply([after, before], phase, (right, zright), 0, away, stay, high, low)


def far_kernel(real, imag, phase, right, zright, away, stay, high, low):
    multiply([Halves(real, imag)], phase, (right, zright), 0, away, stay, high, low)


def add_kernel(*refs):
    x = lax.axis_index("x")
    y = lax.axis_index("y")
    zh = lax.axis_index("zh")
    outs, held = refs[6:10], refs[10]
    order = (((0, 0), (0, 1), (1, 0), (3, 0), (2, 0)), ((1, 1), (3, 1)), ((2, 1),))
    for call_at, blocks in enumerate(order):
        for sub, (distance, came) in enumerate(blocks):
            to = lax.rem(x + distance - y + 4, 4)
            half = 1 - zh if came else zh
            held[to, pl.ds(pl.multiple_of(half * 24, 8), 24)] = refs[2 * call_at][sub] + refs[2 * call_at + 1][sub]
    for step in range(4):
        outs[step][...] = held[step]


def pack_kernel(first, second, third, fourth, out_ref):
    zh = lax.axis_index("zh")
    total = first[...] + second[...] + third[...] + fourth[...]
    for came in range(2):
        pieces = []
        for piece in range(16):
            begin = piece * 48 + came * 24
            pieces.append(total[:, begin:begin + 24])
        packed = jnp.concatenate(pieces, axis=1)
        half = 1 - zh if came else zh
        for zl in range(4):
            for core in range(2):
                for row in range(6):
                    at = zl * 12 + core * 6 + row
                    out_ref[zl * 4 + half * 2 + core, :, row * 384:(row + 1) * 384] = packed[at:at + 1]


def last_kernel(direction_ref, part_ref, out_ref):
    for core in range(2):
        total = part_ref[core]
        for source in range(1, 8):
            total = total + part_ref[2 * source + core]
        total = jnp.concatenate([total[:, row * 384:(row + 1) * 384] for row in range(6)], axis=0)
        for p in range(2):
            for reim in range(2):
                begin = p * 192 + reim * 96
                fields = [total[:, begin + 24 * k:begin + 24 * k + 24] for k in range(4)]
                out_ref[2 * core + p, 0, reim] = fields[0]
                for d in range(1, 4):
                    k = direction_ref[d - 1]
                    value = jnp.where(k == 1, fields[2], fields[1])
                    out_ref[2 * core + p, d, reim] = jnp.where(k == 2, fields[3], value)


def vmem(count):
    return [pl.BlockSpec(memory_space=pltpu.VMEM)] * count


def call(kernel, name, outs, operands, scratch=(), scalars=0, micros=1):
    out_shape = tuple(
        jax.ShapeDtypeStruct(shape, jnp.bfloat16 if shape[-1] == DEPTH else jnp.float32) for shape in outs
    )
    return pl.pallas_call(
        kernel,
        out_shape=out_shape,
        in_specs=[pl.BlockSpec(memory_space=pltpu.SMEM)] * scalars + vmem(len(operands) - scalars),
        out_specs=tuple(vmem(len(outs))),
        scratch_shapes=list(scratch),
        compiler_params=pltpu.CompilerParams(vmem_limit_bytes=VMEM_BYTES),
        cost_estimate=pl.CostEstimate(
            flops=int(micros * 0.3e9), bytes_accessed=int(micros * 0.3 * 3.0e6), transcendentals=0
        ),
        name=name,
    )(*operands)


def along(value, axis, step):
    count = lax.axis_size(axis)
    return lax.ppermute(value, axis, [(i, (i + step) % count) for i in range(count)])


def left_scratch(count):
    return [pltpu.VMEM((192 * count, DEPTH), jnp.bfloat16)] * 2


def local(eigvecs, links, momenta, directions):
    flat = (ROWS, 128)
    keep, send, halo = call(
        cut_kernel, "cut", [flat, (ROWS + 72, 128), (72, 128)], (eigvecs.reshape(144, 2304),)
    )
    came = along(send, "zh", 1)
    keep_after = along(keep, "x", -1)
    keep_before = along(keep, "x", 1)
    phase, = call(phase_kernel, "phase", [(TILES, 8, 128)], (momenta,), (), 1)
    link, = call(link_kernel, "link", [(TILES, 56, 128)], (links.reshape(54, 2304),))
    first, second, link, phase = lax.optimization_barrier((keep_after[:648], keep_before[648:], link, phase))
    keep_far = (along(first, "x", -1), along(second, "x", 1))
    came, keep_after, keep_before, keep_far, later = lax.optimization_barrier(
        (came, keep_after, keep_before, keep_far, keep)
    )
    zcame = along(came, SITE, -1)
    zkeep = along(later, SITE, -1)
    came_after = along(came, "x", -1)
    came_before = along(came, "x", 1)

    def parts(count):
        return [(count, 24, 768)] * 2

    right, *own = call(
        own_kernel, "own", [(576, DEPTH)] + parts(2) + [(384, DEPTH)] * 2, (keep, came, halo, link, phase), (), 0, 6,
    )
    kept = call(
        kept_kernel, "kept", parts(3) + [(576, DEPTH)] * 2,
        (keep_after, keep_before, *keep_far, phase, right), (), 0, 6,
    )
    half = (648, 128)
    first, second = call(forward_kernel, "forward", [half, half], (came_after, came_before, kept[0]))
    came_far = (along(first, "x", -1), along(second, "x", 1))
    zright, away, stay = call(
        z_kernel, "zfield", [(192, DEPTH)] + parts(5), (*own, *kept, zkeep, zcame, link), (), 0, 5
    )
    products = [(away, stay)]
    products.append(call(
        came_kernel, "came", parts(2), (came_after, came_before, phase, right, zright), left_scratch(2), 0, 4,
    ))
    products.append(call(
        far_kernel, "far", parts(1), (*came_far, phase, right, zright), left_scratch(1), 0, 3
    ))
    terms = []
    for away, stay in products:
        terms += [stay, along(away, "core", 1)]
    ready = call(add_kernel, "add", [(48, 768)] * 4, terms, [pltpu.VMEM((4, 48, 768), jnp.float32)])
    sums = [ready[0]] + [along(ready[step], "y", step) for step in range(1, 4)]
    packed, = call(pack_kernel, "pack", [(16, 1, 2304)], sums)
    mixed = lax.all_to_all(packed, ("zl", "zh", "core"), 0, 0)
    return call(last_kernel, "last", [(4, 4, 2, 6, 24)], (directions, mixed), (), 1)[0]


def solution(mesh):
    fine = Mesh(mesh.devices.reshape(4, 4, 2, 4, 2), ("y", "zl", "core", "x", "zh"))
    ev = ("x", "zh")
    in_specs = (P(None, None, ev, SITE, None), P(None, None, None, None, SITE, None), P(), P())
    out_specs = P(None, None, None, SITE, ev)
    return jax.shard_map(local, mesh=fine, in_specs=in_specs, out_specs=out_specs, check_vma=False)
```

```python
import math

import jax
import jax.numpy as jnp
from jax import lax
from jax.experimental import pallas as pl
from jax.experimental.pallas import tpu as pltpu
from jax.sharding import Mesh
from jax.sharding import PartitionSpec as P

LY = 48
HALF = 1152
TILES = 9
ROWS = 1296
DEPTH = 3456
SITE = ("y", "zl", "core")
VMEM_BYTES = 26 * 1024 * 1024


def cut_kernel(vec_ref, keep_ref, send_ref, halo_ref):
    zh = lax.axis_index("zh")
    for out_ref, other_ref, begin in ((keep_ref, send_ref.at[ROWS:], zh), (send_ref, halo_ref, 1 - zh)):
        for tile in range(TILES):
            at = pl.ds(pl.multiple_of(begin * HALF + tile * 128, 128), 128)
            for reim in range(2):
                row = reim * 648 + tile * 72
                out_ref[row:row + 72] = vec_ref[reim * 72:reim * 72 + 72, at]
        lane = lax.broadcasted_iota(jnp.int32, (24, 128), 1)
        at = pl.ds(pl.multiple_of(begin * HALF, 128), 128)
        for pair in range(3):
            even = vec_ref[pair * 48:pair * 48 + 24, at]
            odd = vec_ref[pair * 48 + 24:pair * 48 + 48, at]
            other_ref[pair * 24:pair * 24 + 24] = jnp.where(lane < LY, even, pltpu.roll(odd, LY, 1))

def link_kernel(link_ref, out_ref):
    zh = lax.axis_index("zh")
    for tile in range(TILES):
        at = pl.ds(pl.multiple_of(zh * HALF + tile * 128, 128), 128)
        out_ref[tile, :54] = link_ref[:, at]


def wrapped(value, period):
    rest = lax.rem(value, period)
    return jnp.where(rest < 0, rest + period, rest)


def phase_kernel(mom_ref, out_ref):
    core = lax.axis_index("core")
    zpos = lax.axis_index("y") * 8 + lax.axis_index("zl") * 2 + core
    row = lax.broadcasted_iota(jnp.int32, (40, 128), 0)
    site = lax.broadcasted_iota(jnp.int32, (40, 128), 1) + 128 * (row >> 2)
    line = jnp.floor((site.astype(jnp.float32) + 0.5) * (1.0 / LY)).astype(jnp.int32)
    momentum = []
    for axis in range(3):
        value = jnp.zeros((40, 128), jnp.int32)
        for index in range(4):
            p = (2 * (1 - core) if index < 2 else 2 * core) + index % 2
            value = jnp.where((row & 3) == index, mom_ref[p, axis], value)
        momentum.append(value)
    fx = wrapped(momentum[0] * (line + 24 * lax.axis_index("zh")), 48).astype(jnp.float32) / 48
    fy = wrapped(momentum[1] * (site - line * LY), 48).astype(jnp.float32) / 48
    fz = wrapped(momentum[2] * zpos, 32).astype(jnp.float32) / 32
    theta = (2.0 * math.pi) * (fx + fy + fz)
    cosines = jnp.cos(theta)
    sines = jnp.sin(theta)
    for tile in range(TILES):
        out_ref[tile, :4] = cosines[4 * tile:4 * tile + 4]
        out_ref[tile, 4:] = sines[4 * tile:4 * tile + 4]


def split(value):
    high = value.astype(jnp.bfloat16)
    return high, (value - high.astype(jnp.float32)).astype(jnp.bfloat16)


def load(first_ref, second_ref, reim, tile, color):
    row = reim * 648 + tile * 72 + color * 24
    return jnp.concatenate([first_ref[row:row + 24], second_ref[row:row + 24]], axis=0)


def put(right_ref, fields, reim, k, tile, color, value):
    row = (reim * fields + k) * 48
    column = (tile * 3 + color) * 128
    high, low = split(value)
    right_ref[row:row + 48, column:column + 128] = high
    right_ref[96 * fields + row:96 * fields + row + 48, column:column + 128] = low


def transport(right_ref, fields, k, tile, far, link_ref, direction):
    for row in range(3):
        re = None
        im = None
        for column in range(3):
            at = direction * 18 + row * 3 + column
            ur = link_ref[tile, at:at + 1, :]
            ui = link_ref[tile, at + 9:at + 10, :]
            more_re = ur * far[0][column] - ui * far[1][column]
            more_im = ur * far[1][column] + ui * far[0][column]
            re = more_re if re is None else re + more_re
            im = more_im if im is None else im + more_im
        put(right_ref, fields, 0, k, tile, row, re)
        put(right_ref, fields, 1, k, tile, row, im)


def build_plane(keep_ref, came_ref, halo_ref, link_ref, right_ref):
    lane = lax.broadcasted_iota(jnp.int32, (48, 128), 1)

    def beyond_x(reim, tile, color):
        here = pltpu.roll(load(keep_ref, came_ref, reim, tile, color), 80, 1)
        if tile + 1 < TILES:
            after = pltpu.roll(load(keep_ref, came_ref, reim, tile + 1, color), 80, 1)
        else:
            field = reim * 3 + color
            row = field // 2 * 24
            at = ROWS + row
            after = jnp.concatenate([halo_ref[row:row + 24], came_ref[at:at + 24]], axis=0)
            after = pltpu.roll(after, 80 - LY * (field % 2), 1)
        return jnp.where(lane < 80, here, after)

    def beyond_y(reim, tile, color):
        here = load(keep_ref, came_ref, reim, tile, color)
        value = pltpu.roll(here, 127, 1)
        back = pltpu.roll(here, 47, 1)
        for at in range(128):
            if (tile * 128 + at) % LY == LY - 1:
                if at >= 47:
                    value = jnp.where(lane == at, back, value)
                else:
                    before = pltpu.roll(load(keep_ref, came_ref, reim, tile - 1, color), 47, 1)
                    value = jnp.where(lane == at, before, value)
        if (tile * 128 + 127) % LY != LY - 1:
            after = pltpu.roll(load(keep_ref, came_ref, reim, tile + 1, color), 127, 1)
            value = jnp.where(lane == 127, after, value)
        return value

    def build(tile):
        for color in range(3):
            for reim in range(2):
                put(right_ref, 3, reim, 0, tile, color, load(keep_ref, came_ref, reim, tile, color))
        for direction, beyond in enumerate((beyond_x, beyond_y)):
            far = [[beyond(reim, tile, color) for color in range(3)] for reim in range(2)]
            transport(right_ref, 3, direction + 1, tile, far, link_ref, direction)

    return build


def build_z(zkeep_ref, zcame_ref, link_ref, right_ref):
    def build(tile):
        far = [[load(zkeep_ref, zcame_ref, reim, tile, color) for color in range(3)] for reim in range(2)]
        transport(right_ref, 1, 0, tile, far, link_ref, 2)

    return build


def make_left(blocks, phase_ref, high_ref, low_ref, tile):
    rows = 24 * len(blocks)
    for index in range(4):
        cosv = phase_ref[tile, index:index + 1, :]
        sinv = phase_ref[tile, 4 + index:5 + index, :]
        for color in range(3):
            row = tile * 72 + color * 24
            left_real = []
            left_imag = []
            for block in blocks:
                a = block[row:row + 24]
                b = block[row + 648:row + 672]
                left_real.append(a * cosv - b * sinv)
                left_imag.append(-(a * sinv + b * cosv))
            high, low = split(jnp.concatenate(left_real + left_imag, axis=0))
            column = tile * 384 + color * 128
            high_ref[2 * rows * index:2 * rows * (index + 1), column:column + 128] = high
            low_ref[2 * rows * index:2 * rows * (index + 1), column:column + 128] = low


def multiply(blocks, phase_ref, rights, first, away_ref, stay_ref, high_ref, low_ref, build=None, offset=0):
    count = len(blocks)
    rows = 24 * count
    bounds = (0, TILES) if blocks[0] is None else (0, 2, 6, TILES)

    def prepare(chunk):
        for tile in range(bounds[chunk], bounds[chunk + 1]):
            if build is not None:
                build(tile)
            make_left(blocks, phase_ref, high_ref, low_ref, tile)

    def times(left, right):
        return lax.dot_general(
            left, right, (((1,), (1,)), ((), ())), preferred_element_type=jnp.float32
        )

    def joined(parts):
        return parts[0] if len(parts) == 1 else jnp.concatenate(parts, axis=0)

    widths = [ref.shape[0] // 4 for ref in rights]
    count_high = 2 * sum(widths)
    if blocks[0] is not None:
        prepare(0)
    total = None
    for chunk in range(len(bounds) - 1):
        if chunk + 2 < len(bounds) and blocks[0] is not None:
            prepare(chunk + 1)
        part = slice(bounds[chunk] * 384, bounds[chunk + 1] * 384)
        highs = [ref[:2 * width, part] for ref, width in zip(rights, widths)]
        lows = [ref[2 * width:, part] for ref, width in zip(rights, widths)]
        both = times(high_ref[:, part], joined(highs + lows))
        more = both[:, :count_high] + both[:, count_high:] + times(low_ref[:, part], joined(highs))
        total = more if total is None else total + more
    for index in range(4):
        out_ref = (away_ref, stay_ref)[index // 2]
        base = 2 * rows * index
        top = total[base:base + rows]
        low = total[base + rows:base + 2 * rows]
        begin = 0
        to = first * 48
        for width in widths:
            mid = begin + width
            end = mid + width
            product = (top[:, begin:mid] - low[:, mid:end], low[:, begin:mid] + top[:, mid:end])
            for reim in range(2):
                column = (2 * (index % 2) + reim) * 192 + to
                for sub in range(count):
                    out_ref[offset + sub, :, column:column + width] = product[reim][sub * 24:sub * 24 + 24]
            begin = end
            to += width


def own_kernel(keep, came, halo, link, phase, token, right, away, stay, high, low):
    build = build_plane(keep, came, halo, link, right)
    multiply([keep, came], phase, (right,), 0, away, stay, high, low, build)


def left_kernel(after, before, real, imag, phase_ref, high_ref, low_ref, token_ref):
    blocks = [after, before, Halves(real, imag)]
    for tile in range(TILES):
        make_left(blocks, phase_ref, high_ref, low_ref, tile)
    token_ref[...] = phase_ref[0] + phase_ref[1]


def kept_kernel(high, low, right, away, stay):
    multiply([None] * 3, None, (right,), 0, away, stay, high, low)


def z_kernel(
    own_away, own_stay, own_high, own_low, kept_away, kept_stay, kept_high, kept_low,
    zkeep, zcame, link, zright, away, stay,
):
    away[:2] = own_away[...]
    away[2:] = kept_away[...]
    stay[:2] = own_stay[...]
    stay[2:] = kept_stay[...]
    build = build_z(zkeep, zcame, link, zright)
    for tile in range(TILES):
        build(tile)
    multiply([None] * 2, None, (zright,), 3, away, stay, own_high, own_low)
    multiply([None] * 3, None, (zright,), 3, away, stay, kept_high, kept_low, offset=2)


def forward_kernel(after, before, away, first, second):
    first[...] = after[:648]
    second[...] = before[648:ROWS]


class Halves:
    def __init__(self, real, imag):
        self.parts = (real, imag)

    def __getitem__(self, rows):
        return self.parts[rows.start // 648][rows.start % 648:rows.start % 648 + 24]


def came_kernel(after, before, phase, right, zright, away, stay, high, low):
    multiply([after, before], phase, (right, zright), 0, away, stay, high, low)


def far_kernel(real, imag, phase, right, zright, away, stay, high, low):
    multiply([Halves(real, imag)], phase, (right, zright), 0, away, stay, high, low)


def add_kernel(*refs):
    x = lax.axis_index("x")
    y = lax.axis_index("y")
    zh = lax.axis_index("zh")
    outs, held = refs[6:10], refs[10]
    order = (((0, 0), (0, 1), (1, 0), (3, 0), (2, 0)), ((1, 1), (3, 1)), ((2, 1),))
    for call_at, blocks in enumerate(order):
        for sub, (distance, came) in enumerate(blocks):
            to = lax.rem(x + distance - y + 4, 4)
            half = 1 - zh if came else zh
            held[to, pl.ds(pl.multiple_of(half * 24, 8), 24)] = refs[2 * call_at][sub] + refs[2 * call_at + 1][sub]
    for step in range(4):
        outs[step][...] = held[step]


def pack_kernel(first, second, third, fourth, out_ref):
    zh = lax.axis_index("zh")
    total = first[...] + second[...] + third[...] + fourth[...]
    for came in range(2):
        pieces = []
        for piece in range(16):
            begin = piece * 48 + came * 24
            pieces.append(total[:, begin:begin + 24])
        packed = jnp.concatenate(pieces, axis=1)
        half = 1 - zh if came else zh
        for zl in range(4):
            for core in range(2):
                for row in range(6):
                    at = zl * 12 + core * 6 + row
                    out_ref[zl * 4 + half * 2 + core, :, row * 384:(row + 1) * 384] = packed[at:at + 1]


def last_kernel(direction_ref, part_ref, out_ref):
    for core in range(2):
        total = part_ref[core]
        for source in range(1, 8):
            total = total + part_ref[2 * source + core]
        total = jnp.concatenate([total[:, row * 384:(row + 1) * 384] for row in range(6)], axis=0)
        for p in range(2):
            for reim in range(2):
                begin = p * 192 + reim * 96
                fields = [total[:, begin + 24 * k:begin + 24 * k + 24] for k in range(4)]
                out_ref[2 * core + p, 0, reim] = fields[0]
                for d in range(1, 4):
                    k = direction_ref[d - 1]
                    value = jnp.where(k == 1, fields[2], fields[1])
                    out_ref[2 * core + p, d, reim] = jnp.where(k == 2, fields[3], value)


def vmem(count):
    return [pl.BlockSpec(memory_space=pltpu.VMEM)] * count


def call(kernel, name, outs, operands, scratch=(), scalars=0, micros=1):
    out_shape = tuple(
        jax.ShapeDtypeStruct(shape, jnp.bfloat16 if shape[-1] == DEPTH else jnp.float32) for shape in outs
    )
    return pl.pallas_call(
        kernel,
        out_shape=out_shape,
        in_specs=[pl.BlockSpec(memory_space=pltpu.SMEM)] * scalars + vmem(len(operands) - scalars),
        out_specs=tuple(vmem(len(outs))),
        scratch_shapes=list(scratch),
        compiler_params=pltpu.CompilerParams(vmem_limit_bytes=VMEM_BYTES),
        cost_estimate=pl.CostEstimate(
            flops=int(micros * 0.3e9), bytes_accessed=int(micros * 0.3 * 3.0e6), transcendentals=0
        ),
        name=name,
    )(*operands)


def along(value, axis, step):
    count = lax.axis_size(axis)
    return lax.ppermute(value, axis, [(i, (i + step) % count) for i in range(count)])


def left_scratch(count):
    return [pltpu.VMEM((192 * count, DEPTH), jnp.bfloat16)] * 2


def local(eigvecs, links, momenta, directions):
    flat = (ROWS, 128)
    keep, send, halo = call(
        cut_kernel, "cut", [flat, (ROWS + 72, 128), (72, 128)], (eigvecs.reshape(144, 2304),)
    )
    came = along(send, "zh", 1)
    keep_after = along(keep, "x", -1)
    keep_before = along(keep, "x", 1)
    phase, = call(phase_kernel, "phase", [(TILES, 8, 128)], (momenta,), (), 1)
    link, = call(link_kernel, "link", [(TILES, 56, 128)], (links.reshape(54, 2304),))
    first, second, link, phase = lax.optimization_barrier((keep_after[:648], keep_before[648:], link, phase))
    keep_far = (along(first, "x", -1), along(second, "x", 1))
    kept_high, kept_low, token = call(
        left_kernel, "left", [(576, DEPTH)] * 2 + [(8, 128)], (keep_after, keep_before, *keep_far, phase)
    )
    came, later, token = lax.optimization_barrier((came, keep, token))
    zcame = along(came, SITE, -1)
    zkeep = along(later, SITE, -1)
    came_after = along(came, "x", -1)
    came_before = along(came, "x", 1)

    def parts(count):
        return [(count, 24, 768)] * 2

    right, *own = call(
        own_kernel, "own", [(576, DEPTH)] + parts(2) + [(384, DEPTH)] * 2, (keep, came, halo, link, phase, token), (), 0, 6,
    )
    kept = call(kept_kernel, "kept", parts(3), (kept_high, kept_low, right), (), 0, 6)
    half = (648, 128)
    first, second = call(forward_kernel, "forward", [half, half], (came_after, came_before, kept[0]))
    came_far = (along(first, "x", -1), along(second, "x", 1))
    zright, away, stay = call(
        z_kernel, "zfield", [(192, DEPTH)] + parts(5), (*own, *kept, kept_high, kept_low, zkeep, zcame, link), (), 0, 5
    )
    products = [(away, stay)]
    products.append(call(
        came_kernel, "came", parts(2), (came_after, came_before, phase, right, zright), left_scratch(2), 0, 4,
    ))
    products.append(call(
        far_kernel, "far", parts(1), (*came_far, phase, right, zright), left_scratch(1), 0, 3
    ))
    terms = []
    for away, stay in products:
        terms += [stay, along(away, "core", 1)]
    ready = call(add_kernel, "add", [(48, 768)] * 4, terms, [pltpu.VMEM((4, 48, 768), jnp.float32)])
    sums = [ready[0]] + [along(ready[step], "y", step) for step in range(1, 4)]
    packed, = call(pack_kernel, "pack", [(16, 1, 2304)], sums)
    mixed = lax.all_to_all(packed, ("zl", "zh", "core"), 0, 0)
    return call(last_kernel, "last", [(4, 4, 2, 6, 24)], (directions, mixed), (), 1)[0]


def solution(mesh):
    fine = Mesh(mesh.devices.reshape(4, 4, 2, 4, 2), ("y", "zl", "core", "x", "zh"))
    ev = ("x", "zh")
    in_specs = (P(None, None, ev, SITE, None), P(None, None, None, None, SITE, None), P(), P())
    out_specs = P(None, None, None, SITE, ev)
    return jax.shard_map(local, mesh=fine, in_specs=in_specs, out_specs=out_specs, check_vma=False)
```

```python
import math

import jax
import jax.numpy as jnp
from jax import lax
from jax.experimental import pallas as pl
from jax.experimental.pallas import tpu as pltpu
from jax.sharding import Mesh
from jax.sharding import PartitionSpec as P

LY = 48
HALF = 1152
TILES = 9
ROWS = 1296
DEPTH = 3456
SITE = ("y", "zl", "core")
VMEM_BYTES = 26 * 1024 * 1024


def cut_kernel(vec_ref, keep_ref, send_ref, halo_ref):
    zh = lax.axis_index("zh")
    for out_ref, other_ref, begin in ((keep_ref, send_ref.at[ROWS:], zh), (send_ref, halo_ref, 1 - zh)):
        for tile in range(TILES):
            at = pl.ds(pl.multiple_of(begin * HALF + tile * 128, 128), 128)
            for reim in range(2):
                row = reim * 648 + tile * 72
                out_ref[row:row + 72] = vec_ref[reim * 72:reim * 72 + 72, at]
        lane = lax.broadcasted_iota(jnp.int32, (24, 128), 1)
        at = pl.ds(pl.multiple_of(begin * HALF, 128), 128)
        for pair in range(3):
            even = vec_ref[pair * 48:pair * 48 + 24, at]
            odd = vec_ref[pair * 48 + 24:pair * 48 + 48, at]
            other_ref[pair * 24:pair * 24 + 24] = jnp.where(lane < LY, even, pltpu.roll(odd, LY, 1))

def link_kernel(link_ref, out_ref):
    zh = lax.axis_index("zh")
    for tile in range(TILES):
        at = pl.ds(pl.multiple_of(zh * HALF + tile * 128, 128), 128)
        out_ref[tile, :54] = link_ref[:, at]


def wrapped(value, period):
    rest = lax.rem(value, period)
    return jnp.where(rest < 0, rest + period, rest)


def phase_kernel(mom_ref, out_ref):
    core = lax.axis_index("core")
    zpos = lax.axis_index("y") * 8 + lax.axis_index("zl") * 2 + core
    row = lax.broadcasted_iota(jnp.int32, (40, 128), 0)
    site = lax.broadcasted_iota(jnp.int32, (40, 128), 1) + 128 * (row >> 2)
    line = jnp.floor((site.astype(jnp.float32) + 0.5) * (1.0 / LY)).astype(jnp.int32)
    momentum = []
    for axis in range(3):
        value = jnp.zeros((40, 128), jnp.int32)
        for index in range(4):
            p = (2 * (1 - core) if index < 2 else 2 * core) + index % 2
            value = jnp.where((row & 3) == index, mom_ref[p, axis], value)
        momentum.append(value)
    fx = wrapped(momentum[0] * (line + 24 * lax.axis_index("zh")), 48).astype(jnp.float32) / 48
    fy = wrapped(momentum[1] * (site - line * LY), 48).astype(jnp.float32) / 48
    fz = wrapped(momentum[2] * zpos, 32).astype(jnp.float32) / 32
    theta = (2.0 * math.pi) * (fx + fy + fz)
    cosines = jnp.cos(theta)
    sines = jnp.sin(theta)
    for tile in range(TILES):
        out_ref[tile, :4] = cosines[4 * tile:4 * tile + 4]
        out_ref[tile, 4:] = sines[4 * tile:4 * tile + 4]


def split(value):
    high = value.astype(jnp.bfloat16)
    return high, (value - high.astype(jnp.float32)).astype(jnp.bfloat16)


def load(first_ref, second_ref, reim, tile, color):
    row = reim * 648 + tile * 72 + color * 24
    return jnp.concatenate([first_ref[row:row + 24], second_ref[row:row + 24]], axis=0)


def put(right_ref, fields, reim, k, tile, color, value):
    row = (reim * fields + k) * 48
    column = (tile * 3 + color) * 128
    high, low = split(value)
    right_ref[row:row + 48, column:column + 128] = high
    right_ref[96 * fields + row:96 * fields + row + 48, column:column + 128] = low


def transport(right_ref, fields, k, tile, far, link_ref, direction):
    for row in range(3):
        re = None
        im = None
        for column in range(3):
            at = direction * 18 + row * 3 + column
            ur = link_ref[tile, at:at + 1, :]
            ui = link_ref[tile, at + 9:at + 10, :]
            more_re = ur * far[0][column] - ui * far[1][column]
            more_im = ur * far[1][column] + ui * far[0][column]
            re = more_re if re is None else re + more_re
            im = more_im if im is None else im + more_im
        put(right_ref, fields, 0, k, tile, row, re)
        put(right_ref, fields, 1, k, tile, row, im)


def build_plane(keep_ref, came_ref, halo_ref, link_ref, right_ref):
    lane = lax.broadcasted_iota(jnp.int32, (48, 128), 1)

    def beyond_x(reim, tile, color):
        here = pltpu.roll(load(keep_ref, came_ref, reim, tile, color), 80, 1)
        if tile + 1 < TILES:
            after = pltpu.roll(load(keep_ref, came_ref, reim, tile + 1, color), 80, 1)
        else:
            field = reim * 3 + color
            row = field // 2 * 24
            at = ROWS + row
            after = jnp.concatenate([halo_ref[row:row + 24], came_ref[at:at + 24]], axis=0)
            after = pltpu.roll(after, 80 - LY * (field % 2), 1)
        return jnp.where(lane < 80, here, after)

    def beyond_y(reim, tile, color):
        here = load(keep_ref, came_ref, reim, tile, color)
        value = pltpu.roll(here, 127, 1)
        back = pltpu.roll(here, 47, 1)
        for at in range(128):
            if (tile * 128 + at) % LY == LY - 1:
                if at >= 47:
                    value = jnp.where(lane == at, back, value)
                else:
                    before = pltpu.roll(load(keep_ref, came_ref, reim, tile - 1, color), 47, 1)
                    value = jnp.where(lane == at, before, value)
        if (tile * 128 + 127) % LY != LY - 1:
            after = pltpu.roll(load(keep_ref, came_ref, reim, tile + 1, color), 127, 1)
            value = jnp.where(lane == 127, after, value)
        return value

    def build(tile):
        for color in range(3):
            for reim in range(2):
                put(right_ref, 3, reim, 0, tile, color, load(keep_ref, came_ref, reim, tile, color))
        for direction, beyond in enumerate((beyond_x, beyond_y)):
            far = [[beyond(reim, tile, color) for color in range(3)] for reim in range(2)]
            transport(right_ref, 3, direction + 1, tile, far, link_ref, direction)

    return build


def build_z(zkeep_ref, zcame_ref, link_ref, right_ref):
    def build(tile):
        far = [[load(zkeep_ref, zcame_ref, reim, tile, color) for color in range(3)] for reim in range(2)]
        transport(right_ref, 1, 0, tile, far, link_ref, 2)

    return build


def make_left(blocks, phase_ref, high_ref, low_ref, tile):
    rows = 24 * len(blocks)
    for index in range(4):
        cosv = phase_ref[tile, index:index + 1, :]
        sinv = phase_ref[tile, 4 + index:5 + index, :]
        for color in range(3):
            row = tile * 72 + color * 24
            left_real = []
            left_imag = []
            for block in blocks:
                a = block[row:row + 24]
                b = block[row + 648:row + 672]
                left_real.append(a * cosv - b * sinv)
                left_imag.append(-(a * sinv + b * cosv))
            high, low = split(jnp.concatenate(left_real + left_imag, axis=0))
            column = tile * 384 + color * 128
            high_ref[2 * rows * index:2 * rows * (index + 1), column:column + 128] = high
            low_ref[2 * rows * index:2 * rows * (index + 1), column:column + 128] = low


def multiply(blocks, phase_ref, rights, first, away_ref, stay_ref, high_ref, low_ref, build=None, offset=0):
    count = len(blocks)
    rows = 24 * count
    bounds = (0, TILES) if blocks[0] is None else (0, 1, 3, 5, 7, TILES)

    def prepare(chunk):
        for tile in range(bounds[chunk], bounds[chunk + 1]):
            if build is not None:
                build(tile)
            make_left(blocks, phase_ref, high_ref, low_ref, tile)

    def times(left, right):
        return lax.dot_general(
            left, right, (((1,), (1,)), ((), ())), preferred_element_type=jnp.float32
        )

    def joined(parts):
        return parts[0] if len(parts) == 1 else jnp.concatenate(parts, axis=0)

    widths = [ref.shape[0] // 4 for ref in rights]
    count_high = 2 * sum(widths)
    if blocks[0] is not None:
        prepare(0)
    total = None
    for chunk in range(len(bounds) - 1):
        if chunk + 2 < len(bounds) and blocks[0] is not None:
            prepare(chunk + 1)
        part = slice(bounds[chunk] * 384, bounds[chunk + 1] * 384)
        highs = [ref[:2 * width, part] for ref, width in zip(rights, widths)]
        lows = [ref[2 * width:, part] for ref, width in zip(rights, widths)]
        both = times(high_ref[:, part], joined(highs + lows))
        more = both[:, :count_high] + both[:, count_high:] + times(low_ref[:, part], joined(highs))
        total = more if total is None else total + more
    for index in range(4):
        out_ref = (away_ref, stay_ref)[index // 2]
        base = 2 * rows * index
        top = total[base:base + rows]
        low = total[base + rows:base + 2 * rows]
        begin = 0
        to = first * 48
        for width in widths:
            mid = begin + width
            end = mid + width
            product = (top[:, begin:mid] - low[:, mid:end], low[:, begin:mid] + top[:, mid:end])
            for reim in range(2):
                column = (2 * (index % 2) + reim) * 192 + to
                for sub in range(count):
                    out_ref[offset + sub, :, column:column + width] = product[reim][sub * 24:sub * 24 + 24]
            begin = end
            to += width


def own_kernel(keep, came, halo, link, phase, token, right, away, stay, high, low):
    build = build_plane(keep, came, halo, link, right)
    multiply([keep, came], phase, (right,), 0, away, stay, high, low, build)


def left_kernel(after, before, real, imag, phase_ref, high_ref, low_ref, token_ref):
    blocks = [after, before, Halves(real, imag)]
    for tile in range(TILES):
        make_left(blocks, phase_ref, high_ref, low_ref, tile)
    token_ref[...] = phase_ref[0] + phase_ref[1]


def kept_kernel(high, low, right, away, stay):
    multiply([None] * 3, None, (right,), 0, away, stay, high, low)


def z_kernel(
    own_away, own_stay, own_high, own_low, kept_away, kept_stay, kept_high, kept_low,
    zkeep, zcame, link, zright, away, stay,
):
    away[:2] = own_away[...]
    away[2:] = kept_away[...]
    stay[:2] = own_stay[...]
    stay[2:] = kept_stay[...]
    build = build_z(zkeep, zcame, link, zright)
    for tile in range(TILES):
        build(tile)
    multiply([None] * 2, None, (zright,), 3, away, stay, own_high, own_low)
    multiply([None] * 3, None, (zright,), 3, away, stay, kept_high, kept_low, offset=2)


def forward_kernel(after, before, away, first, second):
    first[...] = after[:648]
    second[...] = before[648:ROWS]


class Halves:
    def __init__(self, real, imag):
        self.parts = (real, imag)

    def __getitem__(self, rows):
        return self.parts[rows.start // 648][rows.start % 648:rows.start % 648 + 24]


def came_kernel(after, before, phase, right, zright, away, stay, high, low):
    multiply([after, before], phase, (right, zright), 0, away, stay, high, low)


def far_kernel(real, imag, phase, right, zright, away, stay, high, low):
    multiply([Halves(real, imag)], phase, (right, zright), 0, away, stay, high, low)


def add_kernel(*refs):
    x = lax.axis_index("x")
    y = lax.axis_index("y")
    zh = lax.axis_index("zh")
    outs, held = refs[6:10], refs[10]
    order = (((0, 0), (0, 1), (1, 0), (3, 0), (2, 0)), ((1, 1), (3, 1)), ((2, 1),))
    for call_at, blocks in enumerate(order):
        for sub, (distance, came) in enumerate(blocks):
            to = lax.rem(x + distance - y + 4, 4)
            half = 1 - zh if came else zh
            held[to, pl.ds(pl.multiple_of(half * 24, 8), 24)] = refs[2 * call_at][sub] + refs[2 * call_at + 1][sub]
    for step in range(4):
        outs[step][...] = held[step]


def pack_kernel(first, second, third, fourth, out_ref):
    zh = lax.axis_index("zh")
    total = first[...] + second[...] + third[...] + fourth[...]
    for came in range(2):
        pieces = []
        for piece in range(16):
            begin = piece * 48 + came * 24
            pieces.append(total[:, begin:begin + 24])
        packed = jnp.concatenate(pieces, axis=1)
        half = 1 - zh if came else zh
        for zl in range(4):
            for core in range(2):
                for row in range(6):
                    at = zl * 12 + core * 6 + row
                    out_ref[zl * 4 + half * 2 + core, :, row * 384:(row + 1) * 384] = packed[at:at + 1]


def last_kernel(direction_ref, part_ref, out_ref):
    for core in range(2):
        total = part_ref[core]
        for source in range(1, 8):
            total = total + part_ref[2 * source + core]
        total = jnp.concatenate([total[:, row * 384:(row + 1) * 384] for row in range(6)], axis=0)
        for p in range(2):
            for reim in range(2):
                begin = p * 192 + reim * 96
                fields = [total[:, begin + 24 * k:begin + 24 * k + 24] for k in range(4)]
                out_ref[2 * core + p, 0, reim] = fields[0]
                for d in range(1, 4):
                    k = direction_ref[d - 1]
                    value = jnp.where(k == 1, fields[2], fields[1])
                    out_ref[2 * core + p, d, reim] = jnp.where(k == 2, fields[3], value)


def vmem(count):
    return [pl.BlockSpec(memory_space=pltpu.VMEM)] * count


def call(kernel, name, outs, operands, scratch=(), scalars=0, micros=1):
    out_shape = tuple(
        jax.ShapeDtypeStruct(shape, jnp.bfloat16 if shape[-1] == DEPTH else jnp.float32) for shape in outs
    )
    return pl.pallas_call(
        kernel,
        out_shape=out_shape,
        in_specs=[pl.BlockSpec(memory_space=pltpu.SMEM)] * scalars + vmem(len(operands) - scalars),
        out_specs=tuple(vmem(len(outs))),
        scratch_shapes=list(scratch),
        compiler_params=pltpu.CompilerParams(vmem_limit_bytes=VMEM_BYTES),
        cost_estimate=pl.CostEstimate(
            flops=int(micros * 0.3e9), bytes_accessed=int(micros * 0.3 * 3.0e6), transcendentals=0
        ),
        name=name,
    )(*operands)


def along(value, axis, step):
    count = lax.axis_size(axis)
    return lax.ppermute(value, axis, [(i, (i + step) % count) for i in range(count)])


def left_scratch(count):
    return [pltpu.VMEM((192 * count, DEPTH), jnp.bfloat16)] * 2


def local(eigvecs, links, momenta, directions):
    flat = (ROWS, 128)
    keep, send, halo = call(
        cut_kernel, "cut", [flat, (ROWS + 72, 128), (72, 128)], (eigvecs.reshape(144, 2304),)
    )
    came = along(send, "zh", 1)
    keep_after = along(keep, "x", -1)
    keep_before = along(keep, "x", 1)
    phase, = call(phase_kernel, "phase", [(TILES, 8, 128)], (momenta,), (), 1)
    link, = call(link_kernel, "link", [(TILES, 56, 128)], (links.reshape(54, 2304),))
    first, second, link, phase = lax.optimization_barrier((keep_after[:648], keep_before[648:], link, phase))
    keep_far = (along(first, "x", -1), along(second, "x", 1))
    kept_high, kept_low, token = call(
        left_kernel, "left", [(576, DEPTH)] * 2 + [(8, 128)], (keep_after, keep_before, *keep_far, phase)
    )
    came, later, token = lax.optimization_barrier((came, keep, token))
    zcame = along(came, SITE, -1)
    zkeep = along(later, SITE, -1)
    came_after = along(came, "x", -1)
    came_before = along(came, "x", 1)

    def parts(count):
        return [(count, 24, 768)] * 2

    right, *own = call(
        own_kernel, "own", [(576, DEPTH)] + parts(2) + [(384, DEPTH)] * 2, (keep, came, halo, link, phase, token), (), 0, 6,
    )
    kept = call(kept_kernel, "kept", parts(3), (kept_high, kept_low, right), (), 0, 6)
    half = (648, 128)
    first, second = call(forward_kernel, "forward", [half, half], (came_after, came_before, kept[0]))
    came_far = (along(first, "x", -1), along(second, "x", 1))
    zright, away, stay = call(
        z_kernel, "zfield", [(192, DEPTH)] + parts(5), (*own, *kept, kept_high, kept_low, zkeep, zcame, link), (), 0, 5
    )
    products = [(away, stay)]
    products.append(call(
        came_kernel, "came", parts(2), (came_after, came_before, phase, right, zright), left_scratch(2), 0, 4,
    ))
    products.append(call(
        far_kernel, "far", parts(1), (*came_far, phase, right, zright), left_scratch(1), 0, 3
    ))
    terms = []
    for away, stay in products:
        terms += [stay, along(away, "core", 1)]
    ready = call(add_kernel, "add", [(48, 768)] * 4, terms, [pltpu.VMEM((4, 48, 768), jnp.float32)])
    sums = [ready[0]] + [along(ready[step], "y", step) for step in range(1, 4)]
    packed, = call(pack_kernel, "pack", [(16, 1, 2304)], sums)
    mixed = lax.all_to_all(packed, ("zl", "zh", "core"), 0, 0)
    return call(last_kernel, "last", [(4, 4, 2, 6, 24)], (directions, mixed), (), 1)[0]


def solution(mesh):
    fine = Mesh(mesh.devices.reshape(4, 4, 2, 4, 2), ("y", "zl", "core", "x", "zh"))
    ev = ("x", "zh")
    in_specs = (P(None, None, ev, SITE, None), P(None, None, None, None, SITE, None), P(), P())
    out_specs = P(None, None, None, SITE, ev)
    return jax.shard_map(local, mesh=fine, in_specs=in_specs, out_specs=out_specs, check_vma=False)
```
